256 devices in a mesh: pts: 128 (over z, y, x), rep: 2 (over core).
Axes of the slice: x: 4, y: 4, z: 8, core: 2. Of those that a mesh axis runs over, the one named last changes fastest.
Arguments:
- features: bfloat16 [2, 32768, 512], P('rep', 'pts'), may hold values from -6 to 6
- neighbours: int32 [2, 32768, 27], P('rep', 'pts'), may hold values from 0 to 32768, as said below
- z_to_hilbert: int32 [2, 32768], P('rep', 'pts'), may hold values from 0 to 32767, as said below
- hilbert: int32 [2, 32768], P('rep', 'pts'), may hold values from 0 to 32767, as said below
- conv_kernel: bfloat16 [27, 512], replicated, may hold values from -1.25 to 1.25
- first_gain: float32 [512], replicated, may hold values from 0.1 to 1.9
- second_gain: float32 [512], replicated, may hold values from 0.1 to 1.9
- qkv_weight: bfloat16 [512, 1536], replicated
- out_weight: bfloat16 [512, 512], replicated, may hold values from -0.25 to 0.25
- up_weight: bfloat16 [512, 2048], replicated, may hold values from -0.25 to 0.25
- down_weight: bfloat16 [2048, 512], replicated, may hold values from -0.125 to 0.125
- cotangent: bfloat16 [2, 32768, 512], P('rep', 'pts'), may hold values from -6 to 6
Outputs:
- mixed_rows: bfloat16 [2, 32768, 512], P('rep', 'pts')
- grad_features: bfloat16 [2, 32768, 512], P('rep', 'pts')
- grad_kernel: float32 [27, 512], replicated
- first_gain_grad: float32 [512], replicated
- second_gain_grad: float32 [512], replicated
- qkv_grad: float32 [512, 1536], P('pts')
- out_grad: float32 [512, 512], P('pts')
- up_grad: float32 [512, 2048], P('pts')
- down_grad: float32 [2048, 512], P('pts')
The draws below stay inside these ranges and needn't reach their ends.
Inputs may be any that keep to these rules, and one draw needn't show every extreme that they name: For each scene and point i, neighbours[i, k] is 32768 or a point of the same scene within 32 rows of i in Z order; entry 13 is i itself; entries 0 and 26 are i - 32 and i + 32 where those exist. `z_to_hilbert`: for each scene a permutation. With 256 points a device in both orders, the points of one device go to at most 4 points of any one device, and to exactly 4 of some device; every device sends the same number of points to the device the same number of indices further on, cyclically. `hilbert`: for each scene the inverse permutation of z_to_hilbert.
All inputs are finite; a program needn't handle non-finite values.
Results may differ from the reference program's by a relative error of at most 0.025.
The reference program's roundings to bfloat16 on the way count: a program that leaves them out, or rounds other values in their place, can miss the bound.
Values may be sent and summed in bfloat16 or wider, within the bound.
No kernel may reach another device: no remote copies, remote signals or barrier semaphores. Data moves between devices by JAX's collectives and lax.ppermute only.
A program may use at most 128 MiB of HBM per device.

```python
import math
import jax
import jax.numpy as jnp
from jax import lax

D = 512
HEADS = 32
PATCH = 1024
FFN_WIDTH = 2048
KVOL = 27
HALO = 32
ROWS = 256
TOKENS = 32768
SCENES = 2
N_PTS = 128


def hilbert_plan(key):

    def one_scene(scene_key):
        mean_rows = ROWS // N_PTS
        halfway = N_PTS // 2
        swing = jax.random.randint(jax.random.fold_in(scene_key, 1), (halfway,), -mean_rows, mean_rows + 1)
        peak = jax.random.randint(jax.random.fold_in(scene_key, 2), (), 0, halfway)
        swing = jnp.where(jnp.arange(halfway) == peak, mean_rows, swing)
        counts = jnp.concatenate([mean_rows + swing, mean_rows - swing])
        ends = jnp.cumsum(counts)
        position = jnp.arange(ROWS, dtype=jnp.int32)
        offsets = jnp.sum((position[:, None] >= ends[None, :]).astype(jnp.int32), axis=1)

        def shuffle_rows(sub_key):
            return jax.random.permutation(sub_key, ROWS)
        send_order = jax.vmap(shuffle_rows)(jax.random.split(jax.random.fold_in(scene_key, 3), N_PTS))
        arrive_order = jax.vmap(shuffle_rows)(jax.random.split(jax.random.fold_in(scene_key, 4), N_PTS))
        sender = jnp.arange(N_PTS, dtype=jnp.int32)[:, None]
        target = (sender + offsets[None, :]) % N_PTS
        destination = target * ROWS + arrive_order[target, position[None, :]]
        source = sender * ROWS + send_order
        return jnp.zeros((TOKENS,), jnp.int32).at[source.reshape(-1)].set(destination.reshape(-1).astype(jnp.int32))
    return jax.vmap(one_scene)(jax.random.split(key, SCENES))


def draw_z_to_hilbert(key, part):
    return hilbert_plan(key)


def draw_hilbert(key, part):
    plan = hilbert_plan(key)

    def invert(plan_row):
        return jnp.zeros((TOKENS,), jnp.int32).at[plan_row].set(jnp.arange(TOKENS, dtype=jnp.int32))
    return jax.vmap(invert)(plan)


def draw_neighbours(key, part):
    key = jax.random.fold_in(key, 5)
    shape = (SCENES, TOKENS, KVOL)
    row_ids = jnp.arange(TOKENS, dtype=jnp.int32)[None, :, None]
    column = jnp.arange(KVOL, dtype=jnp.int32)[None, None, :]
    jitter = jax.random.randint(jax.random.fold_in(key, 1), shape, -HALO, HALO + 1)
    jitter = jnp.where(column == 0, -HALO, jitter)
    jitter = jnp.where(column == KVOL - 1, HALO, jitter)
    jitter = jnp.where(column == KVOL // 2, 0, jitter)
    missing = jax.random.randint(jax.random.fold_in(key, 2), shape, 0, 4) == 0
    missing = missing & (column != 0) & (column != KVOL - 1) & (column != KVOL // 2)
    target = row_ids + jitter
    outside = (target < 0) | (target >= TOKENS)
    return jnp.where(missing | outside, TOKENS, target).astype(jnp.int32)


def draw_qkv_weight(key, part):
    key = jax.random.fold_in(key, 11)
    base = jax.random.normal(key, (D, 3 * D), jnp.float32) * D ** (-0.5)
    return base.astype(jnp.bfloat16)


def level_of(own_key, dims, cuts, low, largest):
    level, own = 1.0, jax.random.fold_in(own_key, 6)
    for dim, shards_of in cuts:
        steps = jnp.exp(jax.random.uniform(jax.random.fold_in(own, dim), (shards_of,), jnp.float32, low / len(cuts), largest / len(cuts)))
        level = level * jnp.repeat(steps, dims[dim] // shards_of).reshape([-1 if axis == dim else 1 for axis in range(len(dims))])
    return level


def normal_values(key, dims, width, most, pieces=(), kind=jnp.bfloat16):
    level = level_of(key, dims, pieces, -0.22, 0.18) if pieces else 1.0
    values = jax.random.normal(key, dims, jnp.float32) * width * level
    return jnp.minimum(jnp.maximum(values, -most), most).astype(kind)


def setup_inputs(seed: int = 0) -> dict:
    key_list = jax.random.split(jax.random.key(seed), 13)
    features = normal_values(key_list[0], (SCENES, TOKENS, D), 1.0, 6.0, ((0, 2), (1, 128)))
    neighbours = draw_neighbours(jax.random.fold_in(key_list[12], 71), 0)
    z_to_hilbert = draw_z_to_hilbert(jax.random.fold_in(key_list[12], 71), 0)
    hilbert = draw_hilbert(jax.random.fold_in(key_list[12], 71), 0)
    conv_kernel = normal_values(key_list[4], (KVOL, D), KVOL ** -0.5, 1.25)
    first_gain = jnp.clip(1.0 + 0.18 * jax.random.normal(key_list[5], (D,), jnp.float32), 0.1, 1.9)
    second_gain = jnp.clip(1.0 + 0.18 * jax.random.normal(key_list[6], (D,), jnp.float32), 0.1, 1.9)
    qkv_weight = draw_qkv_weight(jax.random.fold_in(key_list[12], 71), 0)
    out_weight = normal_values(key_list[8], (D, D), D ** -0.5, 0.25)
    up_weight = normal_values(key_list[9], (D, FFN_WIDTH), D ** -0.5, 0.25)
    down_weight = normal_values(key_list[10], (FFN_WIDTH, D), FFN_WIDTH ** -0.5, 0.125)
    cotangent = normal_values(key_list[11], (SCENES, TOKENS, D), 1.0, 6.0, ((0, 2), (1, 128)))
    return dict(features=features, neighbours=neighbours, z_to_hilbert=z_to_hilbert, hilbert=hilbert, conv_kernel=conv_kernel, first_gain=first_gain, second_gain=second_gain, qkv_weight=qkv_weight, out_weight=out_weight, up_weight=up_weight, down_weight=down_weight, cotangent=cotangent)


epsilon = 1e-05
root_half = 0.7071067811865476
gauss_norm = 0.3989422804014327

def rounded(values):
    return lax.optimization_barrier(values.astype(jnp.bfloat16)).astype(jnp.float32)

def normalize(points, gain):
    widened = points.astype(jnp.float32)
    centre = lax.optimization_barrier(jnp.mean(widened, axis=-1, keepdims=True))
    shifted = widened - centre
    scale = lax.rsqrt(lax.optimization_barrier(jnp.mean(shifted * shifted, axis=-1, keepdims=True)) + epsilon)
    normed = shifted * scale
    return (normed, scale, (normed * gain).astype(jnp.bfloat16))

def norm_back(grad_shaped, normed, scale, gain):
    scaled = grad_shaped * gain
    centred = scaled - lax.optimization_barrier(jnp.mean(scaled, axis=-1, keepdims=True))
    return scale * (centred - normed * lax.optimization_barrier(jnp.mean(scaled * normed, axis=-1, keepdims=True)))

def gelu_parts(hidden):
    normal_cdf = 0.5 * (1.0 + lax.erf(hidden * root_half))
    return (hidden * normal_cdf, normal_cdf + hidden * gauss_norm * jnp.exp(-0.5 * hidden * hidden))

def contract(left, right):
    return lax.dot_general(left, right, (((0,), (0,)), ((), ())), preferred_element_type=jnp.float32)

def against(left, right):
    return lax.dot_general(left, right, (((1,), (1,)), ((), ())), preferred_element_type=jnp.float32)

def convolve(padded, indices, kernel):

    def add_offset(running, column):
        picked = jnp.take(padded, lax.dynamic_index_in_dim(indices, column, 1, keepdims=False), axis=0)
        weight_row = lax.dynamic_index_in_dim(kernel, column, 0, keepdims=False).astype(jnp.float32)
        return (running + weight_row * picked.astype(jnp.float32), None)
    start_sum = jnp.zeros((indices.shape[0], padded.shape[1]), jnp.float32)
    result, _ = lax.scan(add_offset, start_sum, jnp.arange(indices.shape[1], dtype=jnp.int32))
    return result

def convolve_back(padded, indices, kernel, grad_points):
    widened = grad_points.astype(jnp.float32)

    def add_offset(running, column):
        chosen = lax.dynamic_index_in_dim(indices, column, 1, keepdims=False)
        picked = jnp.take(padded, chosen, axis=0).astype(jnp.float32)
        partial_value = lax.optimization_barrier(jnp.sum(widened * picked, axis=0))
        weight_row = lax.dynamic_index_in_dim(kernel, column, 0, keepdims=False).astype(jnp.float32)
        return (running.at[chosen].add(weight_row * widened), partial_value)
    start_sum = jnp.zeros(padded.shape, jnp.float32)
    return lax.scan(add_offset, start_sum, jnp.arange(indices.shape[1], dtype=jnp.int32))

def patch_pass(points, incoming, first_gain, second_gain, qkv_weight, out_weight, up_weight, down_weight):
    channels = points.shape[1]
    head_size = channels // HEADS
    factor = head_size ** (-0.5)
    first_normed, first_scale, first_shaped = normalize(points, first_gain)
    qkv = jnp.dot(first_shaped, qkv_weight, preferred_element_type=jnp.float32).astype(jnp.bfloat16)
    per_head = lax.optimization_barrier(qkv).astype(jnp.float32).reshape(PATCH, 3, HEADS, head_size)
    queries, key_rows, values = (per_head[:, 0], per_head[:, 1], per_head[:, 2])
    scores = jnp.einsum('qhe,khe->hqk', queries, key_rows) * factor
    highest = lax.optimization_barrier(jnp.max(scores, axis=-1, keepdims=True))
    exponent = jnp.exp(scores - highest)
    summed = lax.optimization_barrier(jnp.sum(exponent, axis=-1, keepdims=True))
    attention = rounded(exponent / summed)
    attended = jnp.einsum('hqk,khe->qhe', attention, values).reshape(PATCH, channels).astype(jnp.bfloat16)
    between = (points.astype(jnp.float32) + jnp.dot(attended, out_weight, preferred_element_type=jnp.float32)).astype(jnp.bfloat16)
    second_normed, second_scale, second_shaped = normalize(between, second_gain)
    hidden = jnp.dot(second_shaped, up_weight, preferred_element_type=jnp.float32)
    activation, derivative = gelu_parts(hidden)
    activated = activation.astype(jnp.bfloat16)
    mixed_rows = (between.astype(jnp.float32) + jnp.dot(activated, down_weight, preferred_element_type=jnp.float32)).astype(jnp.bfloat16)
    grad_hidden = (against(incoming, down_weight) * derivative).astype(jnp.bfloat16)
    grad_second = against(grad_hidden, up_weight)
    grad_between = (norm_back(grad_second, second_normed, second_scale, second_gain) + incoming.astype(jnp.float32)).astype(jnp.bfloat16)
    upstream = rounded(against(grad_between, out_weight)).reshape(PATCH, HEADS, head_size)
    grad_attention = jnp.einsum('qhe,khe->hqk', upstream, values)
    grad_values = jnp.einsum('hqk,qhe->khe', attention, upstream)
    spread = lax.optimization_barrier(jnp.sum(attention * grad_attention, axis=-1, keepdims=True))
    grad_scores = rounded(attention * (grad_attention - spread) * factor)
    grad_queries = jnp.einsum('hqk,khe->qhe', grad_scores, key_rows)
    grad_keys = jnp.einsum('hqk,qhe->khe', grad_scores, queries)
    grad_qkv = jnp.stack([grad_queries, grad_keys, grad_values], axis=1).reshape(PATCH, 3 * channels).astype(jnp.bfloat16)
    grad_first = against(grad_qkv, qkv_weight)
    grad_points = (norm_back(grad_first, first_normed, first_scale, first_gain) + grad_between.astype(jnp.float32)).astype(jnp.bfloat16)
    partials = (contract(first_shaped, grad_qkv), contract(attended, grad_between), contract(second_shaped, grad_hidden), contract(activated, incoming), lax.optimization_barrier(jnp.sum(grad_first * first_normed, axis=0)), lax.optimization_barrier(jnp.sum(grad_second * second_normed, axis=0)))
    return (mixed_rows, grad_points, partials)

def scene_pass(features, neighbours, z_to_hilbert, hilbert, cotangent, weights):
    conv_kernel, first_gain, second_gain, qkv_weight, out_weight, up_weight, down_weight = weights
    channels = features.shape[1]
    padded = jnp.concatenate([features, jnp.zeros((1, channels), features.dtype)], axis=0)
    merged = (features.astype(jnp.float32) + convolve(padded, neighbours, conv_kernel)).astype(jnp.bfloat16)
    ordered = jnp.take(merged, hilbert, axis=0)

    def one_patch(couple):
        return patch_pass(couple[0], couple[1], first_gain, second_gain, qkv_weight, out_weight, up_weight, down_weight)
    mixed_rows, grad_points, partials = lax.map(one_patch, (ordered.reshape(-1, PATCH, channels), cotangent.reshape(-1, PATCH, channels)))
    grad_merged = jnp.take(grad_points.reshape(-1, channels), z_to_hilbert, axis=0)
    spilled, kernel_part = convolve_back(padded, neighbours, conv_kernel, grad_merged)
    grad_features = (grad_merged.astype(jnp.float32) + spilled[:-1]).astype(jnp.bfloat16)
    summed = tuple((lax.optimization_barrier(jnp.sum(partial_value, axis=0)) for partial_value in partials)) + (kernel_part,)
    return (mixed_rows.reshape(-1, channels), grad_features, summed)

def reference(features, neighbours, z_to_hilbert, hilbert, conv_kernel, first_gain, second_gain, qkv_weight, out_weight, up_weight, down_weight, cotangent):
    weights = (conv_kernel, first_gain, second_gain, qkv_weight, out_weight, up_weight, down_weight)
    results = [scene_pass(features[scene_index], neighbours[scene_index], z_to_hilbert[scene_index], hilbert[scene_index], cotangent[scene_index], weights) for scene_index in range(SCENES)]
    scale = 1.0 / math.sqrt(SCENES * TOKENS)
    mixed_rows = jnp.stack([result[0] for result in results])
    grad_features = jnp.stack([result[1] for result in results])
    totals = [scale * reduce_sum([result[2][member] for result in results]) for member in range(7)]
    return (mixed_rows, grad_features, totals[6], totals[4], totals[5], totals[0], totals[1], totals[2], totals[3])

def reduce_sum(arrays):
    result = arrays[0]
    for another in arrays[1:]:
        result = result + another
    return result
```

```python
import functools
import math

import jax
import jax.numpy as jnp
from jax import lax
from jax.experimental import pallas as pl
from jax.experimental.pallas import tpu as pltpu
from jax.sharding import PartitionSpec as P

HEADS = 32
GROUP = 4
HALO = 32
HEAD = 16

epsilon = 1e-05
root_half = 0.7071067811865476
gauss_norm = 0.3989422804014327

f32 = jnp.float32
bf16 = jnp.bfloat16
MB = 1 << 20


def dot(left, right):
    return jnp.dot(left, right, preferred_element_type=f32)


def against(left, right):
    return lax.dot_general(left, right, (((1,), (1,)), ((), ())), preferred_element_type=f32)


def contract(left, right):
    return lax.dot_general(left, right, (((0,), (0,)), ((), ())), preferred_element_type=f32)


def iota(shape, dim):
    return lax.broadcasted_iota(jnp.int32, shape, dim)


def one_hot(condition):
    return jnp.where(condition, 1.0, 0.0).astype(bf16)


def normalize(widened):
    centre = jnp.mean(widened, axis=-1, keepdims=True)
    shifted = widened - centre
    scale = lax.rsqrt(jnp.mean(shifted * shifted, axis=-1, keepdims=True) + epsilon)
    return shifted * scale, scale


def norm_back(grad_shaped, normed, scale, gain):
    scaled = grad_shaped * gain
    centred = scaled - jnp.mean(scaled, axis=-1, keepdims=True)
    return scale * (centred - normed * jnp.mean(scaled * normed, axis=-1, keepdims=True))


def gelu_parts(hidden):
    normal_cdf = 0.5 * (1.0 + lax.erf(hidden * root_half))
    return (hidden * normal_cdf, normal_cdf + hidden * gauss_norm * jnp.exp(-0.5 * hidden * hidden))


def log2(number):
    return number.bit_length() - 1


def slot_row(row, col, rows, slots):
    peer_row = row >> log2(rows)
    peer_col = col >> log2(rows)
    earlier = (peer_row == peer_col) & (col < row)
    rank = jnp.sum(jnp.where(earlier, 1, 0), axis=0, keepdims=True)
    return peer_row * slots + rank


def slot_col(row, col, rows, slots):
    peer_row = row >> log2(rows)
    peer_col = col >> log2(rows)
    earlier = (peer_row == peer_col) & (row < col)
    rank = jnp.sum(jnp.where(earlier, 1, 0), axis=1, keepdims=True)
    return peer_col * slots + rank


def send_row(row, col, rows, slots):
    peer_row = row >> log2(rows)
    peer_col = col >> log2(rows)
    shape = (col.shape[0], row.shape[1])
    earlier = (peer_row == peer_col) & (iota(shape, 0) < iota(shape, 1))
    rank = jnp.sum(jnp.where(earlier, 1, 0), axis=0, keepdims=True)
    return peer_row * slots + rank


def send_col(row, col, rows, slots):
    peer_row = row >> log2(rows)
    peer_col = col >> log2(rows)
    shape = (col.shape[0], row.shape[1])
    earlier = (peer_row == peer_col) & (iota(shape, 1) < iota(shape, 0))
    rank = jnp.sum(jnp.where(earlier, 1, 0), axis=1, keepdims=True)
    return peer_col * slots + rank


def conv_forward(where_ref, low, own, high, nb, ker, zrow, zcol, out, extended, merged, *, scene):
    rows, channels = own.shape
    block = rows // 2
    span = block + 2 * HALO
    extended[pl.ds(0, HALO), :] = low[...]
    extended[pl.ds(HALO, rows), :] = own[...]
    extended[pl.ds(HALO + rows, HALO), :] = high[...]
    base = where_ref[0] * rows - HALO
    for part in range(2):
        window = extended[pl.ds(block * part, span), :]
        index = nb[pl.ds(block * part, block), :]
        index = jnp.where(index == scene, -1, index - (base + block * part))
        lanes = iota((block, span), 1)
        total = own[pl.ds(block * part, block), :].astype(f32)
        for k in range(nb.shape[1]):
            picked = dot(one_hot(index[:, k : k + 1] == lanes), window)
            total = total + ker[pl.ds(k, 1), :] * picked
        merged[pl.ds(block * part, block), :] = total.astype(bf16)
    slots_all = out.shape[0]
    slots = 2 * rows * rows // scene
    slot = send_row(zrow[...], zcol[...], rows, slots)
    out[...] = dot(one_hot(iota((slots_all, rows), 0) == slot), merged[...]).astype(bf16)


def first_norm(where_ref, arrived, hrow, hcol, gain, weight, perm, ordered, shaped_perm, qkv, *, scene):
    rows, channels = ordered.shape
    slots = 2 * rows * rows // scene
    slot = slot_col(hrow[...], hcol[...], rows, slots)
    points = dot(one_hot(iota((rows, arrived.shape[0]), 1) == slot), arrived[...])
    ordered[...] = points.astype(bf16)
    normed, _ = normalize(points)
    shaped = (normed * gain[...]).astype(bf16)
    shaped_perm[...] = shaped
    result = dot(shaped, weight[...]).astype(bf16)
    here = where_ref[1]
    width = channels // GROUP
    for group in range(GROUP):
        place = lax.rem(group - here + GROUP, GROUP)
        for kind in range(3):
            first = kind * channels + group * width
            qkv[place, :, kind * width : (kind + 1) * width] = result[:, first : first + width]


def attention_forward(b0, b1, b2, b3, probs, out_t, a0, a1, a2, a3, q_all, k_all, v_t):
    head = pl.program_id(0)
    blocks = (b0, b1, b2, b3)
    rows = b0.shape[0]
    width = b0.shape[1] // 3
    keys = rows * GROUP
    factor = HEAD ** (-0.5)

    @pl.when(head == 0)
    def _():
        for place, block in enumerate(blocks):
            here = pl.ds(place * rows, rows)
            q_all[here, :] = (block[:, :width].astype(f32) * factor).astype(bf16)
            k_all[here, :] = block[:, width : 2 * width]
            v_t[:, place * rows : (place + 1) * rows] = block[:, 2 * width :].astype(f32).T.astype(bf16)

    mine = (iota((keys, width), 1) // HEAD) == head
    k_head = jnp.where(mine, k_all[...], jnp.zeros((), bf16))
    at = pl.multiple_of(head * HEAD, HEAD)
    v_head = v_t[pl.ds(at, HEAD), :]
    for part in range(GROUP):
        cols = slice(part * rows, (part + 1) * rows)
        scores = against(k_head, q_all[cols, :])
        highest = jnp.max(scores, axis=0, keepdims=True)
        exponent = jnp.exp(scores - highest)
        inverse = 1.0 / jnp.sum(exponent, axis=0, keepdims=True)
        chance = (exponent * inverse).astype(bf16)
        probs[0, :, cols] = chance
        out_t[pl.ds(at, HEAD), cols] = dot(v_head, chance)

    @pl.when(head == pl.num_programs(0) - 1)
    def _():
        for place, result in enumerate((a0, a1, a2, a3)):
            result[...] = out_t[:, place * rows : (place + 1) * rows].T.astype(bf16)


def attention_backward(
    b0, b1, b2, b3, u0, u1, u2, u3, probs, out_t, g0, g1, g2, g3,
    q_all, k_all, v_all, u_all, k_t, spread_t, dq_t, dk, dv,
):
    head = pl.program_id(0)
    blocks = (b0, b1, b2, b3)
    rows = b0.shape[0]
    width = b0.shape[1] // 3
    keys = rows * GROUP
    factor = HEAD ** (-0.5)

    @pl.when(head == 0)
    def _():
        for place, (block, up) in enumerate(zip(blocks, (u0, u1, u2, u3))):
            here = pl.ds(place * rows, rows)
            cols = slice(place * rows, (place + 1) * rows)
            q_all[here, :] = block[:, :width]
            k_all[here, :] = block[:, width : 2 * width]
            v_all[here, :] = (block[:, 2 * width :].astype(f32) * factor).astype(bf16)
            u_all[here, :] = up[...]
            k_t[:, cols] = block[:, width : 2 * width].astype(f32).T.astype(bf16)
            spread_t[:, cols] = up[...].astype(f32).T * out_t[:, cols] * factor
        dk[...] = jnp.zeros_like(dk)
        dv[...] = jnp.zeros_like(dv)

    mine = (iota((keys, width), 1) // HEAD) == head
    nought = jnp.zeros((), bf16)
    v_head = jnp.where(mine, v_all[...], nought)
    at = pl.multiple_of(head * HEAD, HEAD)
    k_head = k_t[pl.ds(at, HEAD), :]
    for part in range(GROUP):
        cols = slice(part * rows, (part + 1) * rows)
        chance = probs[0, :, cols]
        grad = against(v_head, u_all[cols, :])
        spread = jnp.sum(spread_t[pl.ds(at, HEAD), cols], axis=0, keepdims=True)
        grad_scores = (chance.astype(f32) * (grad - spread)).astype(bf16)
        own = mine[: rows, :]
        dv[...] += dot(chance, jnp.where(own, u_all[cols, :], nought))
        dk[...] += dot(grad_scores, jnp.where(own, q_all[cols, :], nought))
        dq_t[pl.ds(at, HEAD), cols] = dot(k_head, grad_scores)

    @pl.when(head == pl.num_programs(0) - 1)
    def _():
        for place, result in enumerate((g0, g1, g2, g3)):
            here = pl.ds(place * rows, rows)
            result[:, :width] = dq_t[:, place * rows : (place + 1) * rows].T.astype(bf16)
            result[:, width : 2 * width] = dk[here, :].astype(bf16)
            result[:, 2 * width :] = dv[here, :].astype(bf16)


def mlp(
    where_ref, a0, a1, a2, a3, ordered, out_w, gain, cot, up, down, perm,
    mixed, att_perm, shaped_perm, activated, grad_hidden, grad_between, upstream, gain_grad,
    att, between, shaped, normed, scale, sum_mixed, sum_grad,
):
    step = pl.program_id(0)
    rows, channels = ordered.shape
    width = channels // GROUP
    here = where_ref[1]

    @pl.when(step == 0)
    def _():
        for place, block in enumerate((a0, a1, a2, a3)):
            group = lax.rem(here + place, GROUP)
            att[:, pl.ds(pl.multiple_of(group * width, width), width)] = block[...]
        attended = att[...]
        att_perm[...] = attended
        total = (ordered[...].astype(f32) + dot(attended, out_w[...])).astype(bf16).astype(f32)
        between[...] = total
        normed_value, scale_value = normalize(total)
        normed[...] = normed_value
        scale[...] = jnp.broadcast_to(scale_value, scale.shape)
        shaped_value = (normed_value * gain[...]).astype(bf16)
        shaped[...] = shaped_value
        shaped_perm[...] = shaped_value
        sum_mixed[...] = total
        sum_grad[...] = jnp.zeros_like(sum_grad)

    hidden = dot(shaped[...], up[...])
    activation, derivative = gelu_parts(hidden)
    active = activation.astype(bf16)
    activated[...] = active
    sum_mixed[...] += dot(active, down[...])
    back = (against(cot[...], down[...]) * derivative).astype(bf16)
    grad_hidden[...] = back
    sum_grad[...] += against(back, up[...])

    @pl.when(step == pl.num_programs(0) - 1)
    def _():
        mixed[...] = sum_mixed[...].astype(bf16)
        grad_second = sum_grad[...]
        gain_grad[...] = jnp.sum(grad_second * normed[...], axis=0, keepdims=True)
        grad = norm_back(grad_second, normed[...], scale[:, :1], gain[...]) + cot[...].astype(f32)
        grad = grad.astype(bf16)
        grad_between[...] = grad
        result = against(grad, out_w[...]).astype(bf16)
        for group in range(GROUP):
            place = lax.rem(group - here + GROUP, GROUP)
            upstream[place, :, :] = result[:, group * width : (group + 1) * width]


def qkv_backward(
    where_ref, g0, g1, g2, g3, ordered, weight, gain, grad_between, hrow, hcol,
    grad_qkv, homeward, gain_grad, *, scene,
):
    rows, channels = ordered.shape
    width = channels // GROUP
    here = where_ref[1]
    for place, block in enumerate((g0, g1, g2, g3)):
        group = lax.rem(here + place, GROUP)
        for kind in range(3):
            first = pl.multiple_of(kind * channels + group * width, width)
            grad_qkv[:, pl.ds(first, width)] = block[:, kind * width : (kind + 1) * width]
    grad_first = against(grad_qkv[...], weight[...])
    normed, scale = normalize(ordered[...].astype(f32))
    gain_grad[...] = jnp.sum(grad_first * normed, axis=0, keepdims=True)
    grad = norm_back(grad_first, normed, scale, gain[...]) + grad_between[...].astype(f32)
    slots = 2 * rows * rows // scene
    slot = slot_row(hrow[...], hcol[...], rows, slots)
    pick = one_hot(iota((homeward.shape[0], rows), 0) == slot)
    homeward[...] = dot(pick, grad.astype(bf16)).astype(bf16)


def conv_backward(
    where_ref, returned, low, own, high, nb_t, ker, zrow, zcol, rim_low, rim_high, centre, kernel_grad,
    extended, total, *, scene,
):
    rows, channels = own.shape
    extended[pl.ds(0, HALO), :] = low[...].astype(f32)
    extended[pl.ds(HALO, rows), :] = own[...].astype(f32)
    extended[pl.ds(HALO + rows, HALO), :] = high[...].astype(f32)
    slots = 2 * rows * rows // scene
    slot = send_col(zrow[...], zcol[...], rows, slots)
    pick = one_hot(iota((rows, returned.shape[0]), 1) == slot)
    grad_wide = dot(pick, returned[...])
    grad = grad_wide.astype(bf16)
    base = where_ref[0] * rows - HALO
    index = nb_t[...]
    index = jnp.where(index == scene, -1, index - base)
    span = rows + 2 * HALO
    sublanes = iota((span, rows), 0)
    total[...] = jnp.zeros_like(total)
    for k in range(nb_t.shape[0]):
        spread = dot(one_hot(index[k : k + 1, :] == sublanes), grad)
        total[...] += ker[pl.ds(k, 1), :] * spread
        kernel_grad[pl.ds(k, 1), :] = jnp.sum(extended[...] * spread, axis=0, keepdims=True)
    rim_low[...] = total[pl.ds(0, HALO), :]
    rim_high[...] = total[pl.ds(HALO + rows, HALO), :]
    centre[...] = total[pl.ds(HALO, rows), :] + grad_wide


def whole(count):
    return [pl.BlockSpec(memory_space=pltpu.VMEM)] * count


def smem():
    return pl.BlockSpec(memory_space=pltpu.SMEM)


def params(limit):
    return pltpu.CompilerParams(vmem_limit_bytes=limit * MB)


def shape(dims, dtype):
    return jax.ShapeDtypeStruct(dims, dtype)


def moved(value, axis, route):
    return lax.ppermute(value, axis, route)


def around(count, steps):
    return [(p, p // GROUP * GROUP + (p + steps) % GROUP) for p in range(count)]


def on_device(
    features, neighbours, z_to_hilbert, hilbert, conv_kernel, first_gain, second_gain,
    qkv_weight, out_weight, up_weight, down_weight, cotangent,
):
    points = features[0]
    rows, channels = points.shape
    devices = lax.axis_size("pts")
    device = lax.axis_index("pts")
    core = lax.axis_index("rep")
    replicas = lax.axis_size("rep")
    scene = rows * devices
    slots_all = 2 * rows
    width = channels // GROUP
    hidden_width = up_weight.shape[1]
    offsets = neighbours.shape[2]
    patch = rows * GROUP
    group_heads = HEADS // GROUP
    where = jnp.stack([device, device % GROUP]).astype(jnp.int32)
    forward = [(i, i + 1) for i in range(devices - 1)]
    backward = [(i + 1, i) for i in range(devices - 1)]
    low = lax.ppermute(points[rows - HALO :], "pts", forward)
    high = lax.ppermute(points[:HALO], "pts", backward)
    nb = neighbours[0]
    zrow, zcol = z_to_hilbert.reshape(1, rows), z_to_hilbert.reshape(rows, 1)
    hrow, hcol = hilbert.reshape(1, rows), hilbert.reshape(rows, 1)
    gain1, gain2 = first_gain.reshape(1, channels), second_gain.reshape(1, channels)
    kernel_wide = conv_kernel.astype(f32)
    incoming = cotangent[0]
    nothing = jnp.zeros((8, 128), bf16)

    outgoing = pl.pallas_call(
        functools.partial(conv_forward, scene=scene),
        out_shape=shape((slots_all, channels), bf16),
        in_specs=[smem()] + whole(7),
        out_specs=whole(1)[0],
        scratch_shapes=[pltpu.VMEM((rows + 2 * HALO, channels), bf16), pltpu.VMEM((rows, channels), bf16)],
        compiler_params=params(32),
        name="conv_forward",
    )(where, low, points, high, nb, kernel_wide, zrow, zcol)

    def exchange(value):
        cut = value.reshape(devices, slots_all // devices, channels)
        return lax.all_to_all(cut, "pts", split_axis=0, concat_axis=0, tiled=True).reshape(slots_all, channels)

    arrived = exchange(outgoing)

    ordered, shaped1, qkv = pl.pallas_call(
        functools.partial(first_norm, scene=scene),
        out_shape=(
            shape((rows, channels), bf16),
            shape((rows, channels), bf16),
            shape((GROUP, rows, 3 * width), bf16),
        ),
        in_specs=[smem()] + whole(6),
        out_specs=tuple(whole(3)),
        compiler_params=params(32),
        name="first_norm",
    )(where, arrived, hrow, hcol, gain1, qkv_weight, nothing)

    def spread_out(blocks):
        return [blocks[0]] + [moved(blocks[j], "pts", around(devices, j)) for j in range(1, GROUP)]

    def bring_back(blocks):
        return [blocks[0]] + [moved(blocks[j], "pts", around(devices, -j)) for j in range(1, GROUP)]

    blocks = spread_out(qkv)

    def fixed(dims):
        return pl.BlockSpec(dims, lambda i: (0,) * len(dims))

    by_head = pl.BlockSpec((1, patch, patch), lambda i: (i, 0, 0))
    probs, out_t, *attended = pl.pallas_call(
        attention_forward,
        grid=(group_heads,),
        out_shape=(shape((group_heads, patch, patch), bf16), shape((width, patch), f32))
        + (shape((rows, width), bf16),) * GROUP,
        in_specs=[fixed((rows, 3 * width))] * GROUP,
        out_specs=(by_head, fixed((width, patch))) + (fixed((rows, width)),) * GROUP,
        scratch_shapes=[
            pltpu.VMEM((patch, width), bf16),
            pltpu.VMEM((patch, width), bf16),
            pltpu.VMEM((width, patch), bf16),
        ],
        compiler_params=params(48),
        name="attention_forward",
    )(*blocks)

    attended = bring_back(attended)

    chunk = hidden_width // 4
    by_chunk = pl.BlockSpec((rows, chunk), lambda i: (0, i))
    square = fixed((rows, channels))
    (
        mixed_rows, attended_all, shaped2, activated, grad_hidden, grad_between, upstream, second_gain_part,
    ) = pl.pallas_call(
        mlp,
        grid=(4,),
        out_shape=(
            shape((rows, channels), bf16),
            shape((rows, channels), bf16),
            shape((rows, channels), bf16),
            shape((rows, hidden_width), bf16),
            shape((rows, hidden_width), bf16),
            shape((rows, channels), bf16),
            shape((GROUP, rows, width), bf16),
            shape((1, channels), f32),
        ),
        in_specs=[smem()]
        + [fixed((rows, width))] * GROUP
        + [
            square,
            fixed((channels, channels)),
            fixed((1, channels)),
            square,
            pl.BlockSpec((channels, chunk), lambda i: (0, i)),
            pl.BlockSpec((chunk, channels), lambda i: (i, 0)),
            fixed((8, 128)),
        ],
        out_specs=(
            square, square, square, by_chunk, by_chunk, square,
            fixed((GROUP, rows, width)), fixed((1, channels)),
        ),
        scratch_shapes=[
            pltpu.VMEM((rows, channels), bf16),
            pltpu.VMEM((rows, channels), f32),
            pltpu.VMEM((rows, channels), bf16),
            pltpu.VMEM((rows, channels), f32),
            pltpu.VMEM((rows, 128), f32),
            pltpu.VMEM((rows, channels), f32),
            pltpu.VMEM((rows, channels), f32),
        ],
        compiler_params=params(48),
        name="mlp",
    )(where, *attended, ordered, out_weight, gain2, incoming, up_weight, down_weight, nothing)

    upper = spread_out(upstream)

    grads = pl.pallas_call(
        attention_backward,
        grid=(group_heads,),
        out_shape=(shape((rows, 3 * width), bf16),) * GROUP,
        in_specs=[fixed((rows, 3 * width))] * GROUP
        + [fixed((rows, width))] * GROUP
        + [by_head, fixed((width, patch))],
        out_specs=(fixed((rows, 3 * width)),) * GROUP,
        scratch_shapes=[
            pltpu.VMEM((patch, width), bf16),
            pltpu.VMEM((patch, width), bf16),
            pltpu.VMEM((patch, width), bf16),
            pltpu.VMEM((patch, width), bf16),
            pltpu.VMEM((width, patch), bf16),
            pltpu.VMEM((width, patch), f32),
            pltpu.VMEM((width, patch), f32),
            pltpu.VMEM((patch, width), f32),
            pltpu.VMEM((patch, width), f32),
        ],
        compiler_params=params(48),
        name="attention_backward",
    )(*blocks, *upper, probs, out_t)

    grads = bring_back(grads)

    grad_qkv, homeward, first_gain_part = pl.pallas_call(
        functools.partial(qkv_backward, scene=scene),
        out_shape=(
            shape((rows, 3 * channels), bf16),
            shape((slots_all, channels), bf16),
            shape((1, channels), f32),
        ),
        in_specs=[smem()] + whole(10),
        out_specs=tuple(whole(3)),
        compiler_params=params(32),
        name="qkv_backward",
    )(where, *grads, ordered, qkv_weight, gain1, grad_between, hrow, hcol)

    returned = exchange(homeward)

    rim_low, rim_high, centre, kernel_part = pl.pallas_call(
        functools.partial(conv_backward, scene=scene),
        out_shape=(
            shape((HALO, channels), f32),
            shape((HALO, channels), f32),
            shape((rows, channels), f32),
            shape((offsets, channels), f32),
        ),
        in_specs=[smem()] + whole(8),
        out_specs=tuple(whole(4)),
        scratch_shapes=[
            pltpu.VMEM((rows + 2 * HALO, channels), f32),
            pltpu.VMEM((rows + 2 * HALO, channels), f32),
        ],
        compiler_params=params(32),
        name="conv_backward",
    )(where, returned, low, points, high, nb.T, kernel_wide, zrow, zcol)

    from_above = lax.ppermute(rim_low, "pts", backward)
    from_below = lax.ppermute(rim_high, "pts", forward)
    centre = centre.at[:HALO].add(from_below).at[rows - HALO :].add(from_above)
    grad_features = centre.astype(bf16)

    swap = [(0, 1), (1, 0)]

    def halves(value):
        half = value.shape[1] // replicas
        mine = lax.dynamic_slice_in_dim(value, core * half, half, 1)
        theirs = lax.dynamic_slice_in_dim(value, (1 - core) * half, half, 1)
        return mine, theirs

    def products(lefts, rights):
        pairs = [halves(right) for right in rights]
        packed = jnp.concatenate(list(lefts) + [theirs for _, theirs in pairs], axis=1)
        came = lax.ppermute(packed, "rep", swap)
        results, at = [], 0
        other_left = []
        for left in lefts:
            other_left.append(came[:, at : at + left.shape[1]])
            at += left.shape[1]
        for left, other, (mine, theirs) in zip(lefts, other_left, pairs):
            span = theirs.shape[1]
            both_left = jnp.concatenate([left, other], axis=0)
            both_right = jnp.concatenate([mine, came[:, at : at + span]], axis=0)
            at += span
            results.append(contract(both_left, both_right).astype(bf16))
        return results

    def cut(value):
        return value.reshape(devices, GROUP, -1)

    def scattered(value):
        got = lax.all_to_all(value, "pts", split_axis=0, concat_axis=0, tiled=True)
        return jnp.sum(got.astype(f32), axis=0)

    out_half, up_half, down_half = products(
        (attended_all, shaped2, activated), (grad_between, grad_hidden, incoming)
    )
    early = scattered(jnp.concatenate([cut(out_half), cut(up_half), cut(down_half)], axis=2))
    (qkv_half,) = products((shaped1,), (grad_qkv,))
    late = scattered(cut(qkv_half))
    owned = jnp.concatenate([late, early], axis=1)
    other = lax.ppermute(owned, "rep", swap)
    lower = jnp.where(core == 0, owned, other)
    upper_half = jnp.where(core == 0, other, owned)
    scale = 1.0 / math.sqrt(scene * replicas)
    half_qkv, half_out, half_up = 3 * channels // 2, channels // 2, hidden_width // 2
    at1, at2 = half_qkv + half_out, half_qkv + half_out + half_up

    def joined(first, last, count=GROUP):
        parts = [half[:, first:last].reshape(count, -1) for half in (lower, upper_half)]
        return jnp.concatenate(parts, axis=1) * scale

    down_rows = down_weight.shape[0] // devices

    small = jnp.concatenate([kernel_part, first_gain_part, second_gain_part], axis=0)
    for bit in range(log2(devices)):
        small = small + lax.ppermute(small, "pts", [(p, p ^ (1 << bit)) for p in range(devices)])
    small = (small + lax.ppermute(small, "rep", swap)) * scale

    return (
        mixed_rows[None],
        grad_features[None],
        small[:offsets],
        small[offsets],
        small[offsets + 1],
        joined(0, half_qkv),
        joined(half_qkv, at1),
        joined(at1, at2),
        joined(at2, owned.shape[1], down_rows),
    )


def solution(mesh):
    return jax.shard_map(
        on_device,
        mesh=mesh,
        in_specs=(
            P("rep", "pts", None),
            P("rep", "pts", None),
            P("rep", "pts"),
            P("rep", "pts"),
            P(),
            P(),
            P(),
            P(),
            P(),
            P(),
            P(),
            P("rep", "pts", None),
        ),
        out_specs=(
            P("rep", "pts", None),
            P("rep", "pts", None),
            P(),
            P(),
            P(),
            P("pts", None),
            P("pts", None),
            P("pts", None),
            P("pts", None),
        ),
        check_vma=False,
    )
```

```python
import functools
import math

import jax
import jax.numpy as jnp
from jax import lax
from jax.experimental import pallas as pl
from jax.experimental.pallas import tpu as pltpu
from jax.sharding import PartitionSpec as P

HEADS = 32
GROUP = 4
HALO = 32
HEAD = 16
SLOTS = 4

epsilon = 1e-05
root_half = 0.7071067811865476
gauss_norm = 0.3989422804014327

f32 = jnp.float32
bf16 = jnp.bfloat16
MB = 1 << 20


def dot(left, right):
    return jnp.dot(left, right, preferred_element_type=f32)


def against(left, right):
    return lax.dot_general(left, right, (((1,), (1,)), ((), ())), preferred_element_type=f32)


def contract(left, right):
    return lax.dot_general(left, right, (((0,), (0,)), ((), ())), preferred_element_type=f32)


def iota(shape, dim):
    return lax.broadcasted_iota(jnp.int32, shape, dim)


def one_hot(condition):
    return jnp.where(condition, 1.0, 0.0).astype(bf16)


def normalize(widened):
    centre = jnp.mean(widened, axis=-1, keepdims=True)
    shifted = widened - centre
    scale = lax.rsqrt(jnp.mean(shifted * shifted, axis=-1, keepdims=True) + epsilon)
    return shifted * scale, scale


def norm_back(grad_shaped, normed, scale, gain):
    scaled = grad_shaped * gain
    centred = scaled - jnp.mean(scaled, axis=-1, keepdims=True)
    return scale * (centred - normed * jnp.mean(scaled * normed, axis=-1, keepdims=True))


def gelu_parts(hidden):
    normal_cdf = 0.5 * (1.0 + lax.erf(hidden * root_half))
    return (hidden * normal_cdf, normal_cdf + hidden * gauss_norm * jnp.exp(-0.5 * hidden * hidden))


def log2(number):
    return number.bit_length() - 1


def column(row):
    tall = jnp.broadcast_to(row.astype(f32), (128, row.shape[1]))
    return tall.T[:, :1].astype(jnp.int32)


def slots_by(row, rows, along, order):
    peer_row, col = row >> log2(rows), column(row)
    peer_col = col >> log2(rows)
    dims = (col.shape[0], row.shape[1])
    if order:
        before = iota(dims, 0) < iota(dims, 1) if along == 0 else iota(dims, 1) < iota(dims, 0)
    else:
        before = col < row if along == 0 else row < col
    rank = jnp.sum(jnp.where((peer_row == peer_col) & before, 1, 0), axis=along, keepdims=True)
    peer = peer_row if along == 0 else peer_col
    return peer * (2 * SLOTS) + rank


def pack_rows(values, slot):
    rows, channels = values.shape
    half = channels // 2
    stacked = jnp.concatenate([values[:, :half], values[:, half:]], axis=0)
    wanted = jnp.concatenate([slot, slot + SLOTS], axis=1)
    pick = one_hot(iota((4 * rows, 2 * rows), 0) == wanted)
    return dot(pick, stacked).astype(bf16)


def unpack_rows(packed, slot):
    lanes = iota((slot.shape[0], packed.shape[0]), 1)
    parts = [dot(one_hot(lanes == slot + half * SLOTS), packed) for half in range(2)]
    return jnp.concatenate(parts, axis=1)


def conv_forward(where_ref, low, own, high, nb_t, ker, zrow, out, extended, merged, *, scene):
    rows, channels = own.shape
    block = rows // 2
    span = block + 2 * HALO
    offsets = nb_t.shape[0]
    extended[pl.ds(0, HALO), :] = low[...]
    extended[pl.ds(HALO, rows), :] = own[...]
    extended[pl.ds(HALO + rows, HALO), :] = high[...]
    base = where_ref[0] * rows - HALO
    index = jnp.where(nb_t[...] == scene, -(2 * rows), nb_t[...] - base).astype(f32)
    index = jnp.concatenate([index, jnp.zeros((32 - offsets, rows), f32)], axis=0)
    index = index.T.astype(jnp.int32)
    wide = ker[...].astype(f32)
    lanes = iota((block, span), 1)
    for part in range(2):
        window = extended[pl.ds(block * part, span), :]
        near = index[block * part : block * (part + 1), :] - block * part
        total = own[pl.ds(block * part, block), :].astype(f32)
        for k in range(offsets):
            picked = dot(one_hot(near[:, k : k + 1] == lanes), window)
            total = total + wide[k : k + 1, :] * picked
        merged[pl.ds(block * part, block), :] = total.astype(bf16)
    out[...] = pack_rows(merged[...], slots_by(zrow[...], rows, 0, True))


def first_norm(where_ref, arrived, hrow, gain, weight, ordered, shaped_out, qkv):
    rows, channels = ordered.shape
    points = unpack_rows(arrived[...], slots_by(hrow[...], rows, 1, False))
    ordered[...] = points.astype(bf16)
    normed, _ = normalize(points)
    shaped = (normed * gain[...]).astype(bf16)
    shaped_out[...] = shaped
    result = dot(shaped, weight[...]).astype(bf16)
    here = where_ref[1]
    width = channels // GROUP
    for group in range(GROUP):
        place = lax.rem(group - here + GROUP, GROUP)
        for kind in range(3):
            first = kind * channels + group * width
            qkv[place, :, kind * width : (kind + 1) * width] = result[:, first : first + width]


def attention_forward(b0, b1, b2, b3, probs, out_t, a0, a1, a2, a3, q_all, k_all, v_t, bound):
    head = pl.program_id(0)
    blocks = (b0, b1, b2, b3)
    rows = b0.shape[0]
    width = b0.shape[1] // 3
    keys = rows * GROUP
    factor = HEAD ** (-0.5)

    @pl.when(head == 0)
    def _():
        for place, block in enumerate(blocks):
            here = pl.ds(place * rows, rows)
            q_all[here, :] = (block[:, :width].astype(f32) * factor).astype(bf16)
            k_all[here, :] = block[:, width : 2 * width]
            v_t[:, place * rows : (place + 1) * rows] = block[:, 2 * width :].astype(f32).T.astype(bf16)
        groups = one_hot(iota((width, width), 0) // HEAD == iota((width, width), 1))
        lengths = []
        for ref in (q_all, k_all):
            wide = ref[...].astype(f32)
            lengths.append(jnp.max(dot((wide * wide).astype(bf16), groups), axis=0, keepdims=True))
        bound[0] = jnp.max(lengths[0] * lengths[1])

    mine = (iota((keys, width), 1) // HEAD) == head
    k_head = jnp.where(mine, k_all[...], jnp.zeros((), bf16))
    at = pl.multiple_of(head * HEAD, HEAD)
    v_head = v_t[pl.ds(at, HEAD), :]

    def softmax(shifted):
        for part in range(GROUP):
            cols = slice(part * rows, (part + 1) * rows)
            scores = against(k_head, q_all[cols, :])
            if shifted:
                scores = scores - jnp.max(scores, axis=0, keepdims=True)
            exponent = jnp.exp(scores)
            inverse = 1.0 / jnp.sum(exponent, axis=0, keepdims=True)
            chance = (exponent * inverse).astype(bf16)
            probs[0, :, cols] = chance
            out_t[pl.ds(at, HEAD), cols] = dot(v_head, chance)

    calm = bound[0] <= 1500.0

    @pl.when(calm)
    def _():
        softmax(False)

    @pl.when(jnp.logical_not(calm))
    def _():
        softmax(True)

    @pl.when(head == pl.num_programs(0) - 1)
    def _():
        for place, result in enumerate((a0, a1, a2, a3)):
            result[...] = out_t[:, place * rows : (place + 1) * rows].T.astype(bf16)


def attention_backward(
    b0, b1, b2, b3, u0, u1, u2, u3, probs, out_t, g0, g1, g2, g3,
    q_all, k_all, v_all, u_all, k_t, spread_t, dq_t, dk, dv,
):
    head = pl.program_id(0)
    blocks = (b0, b1, b2, b3)
    rows = b0.shape[0]
    width = b0.shape[1] // 3
    keys = rows * GROUP
    factor = HEAD ** (-0.5)

    @pl.when(head == 0)
    def _():
        for place, (block, up) in enumerate(zip(blocks, (u0, u1, u2, u3))):
            here = pl.ds(place * rows, rows)
            cols = slice(place * rows, (place + 1) * rows)
            q_all[here, :] = block[:, :width]
            k_all[here, :] = block[:, width : 2 * width]
            v_all[here, :] = (block[:, 2 * width :].astype(f32) * factor).astype(bf16)
            u_all[here, :] = up[...]
            k_t[:, cols] = block[:, width : 2 * width].astype(f32).T.astype(bf16)
            spread_t[:, cols] = up[...].astype(f32).T * out_t[:, cols] * factor
        dk[...] = jnp.zeros_like(dk)
        dv[...] = jnp.zeros_like(dv)

    mine = (iota((keys, width), 1) // HEAD) == head
    nought = jnp.zeros((), bf16)
    v_head = jnp.where(mine, v_all[...], nought)
    at = pl.multiple_of(head * HEAD, HEAD)
    k_head = k_t[pl.ds(at, HEAD), :]
    for part in range(GROUP):
        cols = slice(part * rows, (part + 1) * rows)
        chance = probs[0, :, cols]
        grad = against(v_head, u_all[cols, :])
        spread = jnp.sum(spread_t[pl.ds(at, HEAD), cols], axis=0, keepdims=True)
        grad_scores = (chance.astype(f32) * (grad - spread)).astype(bf16)
        own = mine[:rows, :]
        dv[...] += dot(chance, jnp.where(own, u_all[cols, :], nought))
        dk[...] += dot(grad_scores, jnp.where(own, q_all[cols, :], nought))
        dq_t[pl.ds(at, HEAD), cols] = dot(k_head, grad_scores)

    @pl.when(head == pl.num_programs(0) - 1)
    def _():
        for place, result in enumerate((g0, g1, g2, g3)):
            here = pl.ds(place * rows, rows)
            result[:, :width] = dq_t[:, place * rows : (place + 1) * rows].T.astype(bf16)
            result[:, width : 2 * width] = dk[here, :].astype(bf16)
            result[:, 2 * width :] = dv[here, :].astype(bf16)


def mlp(
    where_ref, a0, a1, a2, a3, ordered, first_shaped, out_w, gain, cot, up, down,
    mixed, grad_between, upstream, gain_grad, pack, kept,
    between, shaped, normed, scale, sum_mixed, sum_grad,
):
    step = pl.program_id(0)
    rows, channels = ordered.shape
    width = channels // GROUP
    here, core = where_ref[1], where_ref[3]
    chunk = up.shape[1]
    hidden_width = chunk * 4
    right = 3 * channels + hidden_width

    @pl.when(step == 0)
    def _():
        for place, block in enumerate((a0, a1, a2, a3)):
            group = lax.rem(here + place, GROUP)
            pack[:, pl.ds(pl.multiple_of(group * width, width), width)] = block[...]
        attended = pack[:, :channels]
        total = (ordered[...].astype(f32) + dot(attended, out_w[...])).astype(bf16).astype(f32)
        between[...] = total
        normed_value, scale_value = normalize(total)
        normed[...] = normed_value
        scale[...] = jnp.broadcast_to(scale_value, scale.shape)
        shaped_value = (normed_value * gain[...]).astype(bf16)
        shaped[...] = shaped_value
        pack[:, channels : 2 * channels] = shaped_value
        pack[:, 2 * channels + hidden_width : right] = first_shaped[...]
        sum_mixed[...] = total
        sum_grad[...] = jnp.zeros_like(sum_grad)
        half = channels // 2
        at = right + (channels + hidden_width) // 2
        kept[:, (channels + hidden_width) // 2 :] = cot[:, pl.ds(pl.multiple_of(core * half, half), half)]
        pack[:, at:] = cot[:, pl.ds(pl.multiple_of((1 - core) * half, half), half)]

    hidden = dot(shaped[...], up[...])
    activation, derivative = gelu_parts(hidden)
    active = activation.astype(bf16)
    pack[:, pl.ds(pl.multiple_of(2 * channels + step * chunk, chunk), chunk)] = active
    sum_mixed[...] += dot(active, down[...])
    back = (against(cot[...], down[...]) * derivative).astype(bf16)
    sum_grad[...] += against(back, up[...])
    place = channels // 2 + lax.rem(step, 2) * chunk
    owner = step // 2

    @pl.when(owner == core)
    def _():
        kept[:, pl.ds(pl.multiple_of(place, 128), chunk)] = back

    @pl.when(owner != core)
    def _():
        pack[:, pl.ds(pl.multiple_of(right + place, 128), chunk)] = back

    @pl.when(step == pl.num_programs(0) - 1)
    def _():
        mixed[...] = sum_mixed[...].astype(bf16)
        grad_second = sum_grad[...]
        gain_grad[...] = jnp.sum(grad_second * normed[...], axis=0, keepdims=True)
        grad = norm_back(grad_second, normed[...], scale[:, :1], gain[...]) + cot[...].astype(f32)
        grad = grad.astype(bf16)
        grad_between[...] = grad
        half = channels // 2
        kept[:, :half] = grad_between[:, pl.ds(pl.multiple_of(core * half, half), half)]
        pack[:, right : right + half] = grad_between[:, pl.ds(pl.multiple_of((1 - core) * half, half), half)]
        result = against(grad, out_w[...]).astype(bf16)
        for group in range(GROUP):
            place = lax.rem(group - here + GROUP, GROUP)
            upstream[place, :, :] = result[:, group * width : (group + 1) * width]


def qkv_backward(
    where_ref, g0, g1, g2, g3, ordered, weight, gain, grad_between, hrow,
    kept, sent, homeward, gain_grad, grad_qkv,
):
    rows, channels = ordered.shape
    width = channels // GROUP
    here, core = where_ref[1], where_ref[3]
    for place, block in enumerate((g0, g1, g2, g3)):
        group = lax.rem(here + place, GROUP)
        for kind in range(3):
            first = pl.multiple_of(kind * channels + group * width, width)
            grad_qkv[:, pl.ds(first, width)] = block[:, kind * width : (kind + 1) * width]
    grad_first = against(grad_qkv[...], weight[...])
    normed, scale = normalize(ordered[...].astype(f32))
    gain_grad[...] = jnp.sum(grad_first * normed, axis=0, keepdims=True)
    grad = norm_back(grad_first, normed, scale, gain[...]) + grad_between[...].astype(f32)
    homeward[...] = pack_rows(grad.astype(bf16), slots_by(hrow[...], rows, 0, False))
    half = 3 * channels // 2
    kept[...] = grad_qkv[:, pl.ds(pl.multiple_of(core * half, 128), half)]
    sent[...] = grad_qkv[:, pl.ds(pl.multiple_of((1 - core) * half, 128), half)]


def fold_rows(product):
    rows, columns = product.shape
    half = columns // 2
    tiles = product.reshape(rows // 8, 8, columns)
    turned = pltpu.roll(tiles, 4, 1)
    above = iota((rows // 8, 8, half), 1) < 4
    even = jnp.where(above, tiles[:, :, :half], turned[:, :, half:])
    odd = jnp.where(above, turned[:, :, :half], tiles[:, :, half:])
    return even, odd


def place_folded(out, folded, first, chunk, here):
    even, odd = folded
    span = even.shape[2]
    for level in range(2):
        for y in range(GROUP):
            place = lax.rem(y - here + GROUP, GROUP)
            q = level * 8 + y * 2
            tall = jnp.concatenate([even[q], odd[q], even[q + 1], odd[q + 1]], axis=0)
            at = (2 * chunk + level) * 32
            out[place, at : at + 32, first : first + span] = tall.astype(bf16)


def early_products(where_ref, pack, kept, came, out, *, channels):
    here = where_ref[2]
    hidden_width = pack.shape[1] - kept.shape[1] - 3 * channels
    right = 3 * channels + hidden_width
    half_out, half_up = channels // 2, hidden_width // 2

    def product(left, first, span):
        return contract(pack[:, left], kept[:, first : first + span]) + contract(
            came[:, left], came[:, right + first : right + first + span]
        )

    for chunk in range(4):
        at = chunk * 128
        part = product(slice(at, at + 128), 0, half_out)
        place_folded(out, fold_rows(part), 0, chunk, here)
        part = product(slice(channels + at, channels + at + 128), half_out, half_up)
        place_folded(out, fold_rows(part), half_out // 2, chunk, here)
        at = 2 * channels + chunk * 512
        part = product(slice(at, at + 512), half_out + half_up, half_out)
        tiles = part.reshape(32, 2, 8, half_out)
        first = (half_out + half_up) // 2
        for level in range(2):
            for y in range(GROUP):
                place = lax.rem(y - here + GROUP, GROUP)
                q = level * 16 + y * 4
                row = (2 * chunk + level) * 32
                for side in range(2):
                    flat = tiles[q : q + 4, side].reshape(32, half_out).astype(bf16)
                    out[place, row : row + 32, first + side * half_out : first + (side + 1) * half_out] = flat


def late_products(where_ref, pack, came_pack, kept, came, out, *, channels):
    here = where_ref[2]
    first = pack.shape[1] - 3 * channels
    for chunk in range(4):
        at = slice(chunk * 128, chunk * 128 + 128)
        part = contract(pack[:, at], kept[...]) + contract(came_pack[:, at], came[...])
        place_folded(out, fold_rows(part), 0, chunk, here)


def conv_backward(
    where_ref, returned, low, own, high, nb_t, ker, zrow, rim_low, rim_high, centre, kernel_grad,
    extended, total, *, scene,
):
    rows, channels = own.shape
    extended[pl.ds(0, HALO), :] = low[...].astype(f32)
    extended[pl.ds(HALO, rows), :] = own[...].astype(f32)
    extended[pl.ds(HALO + rows, HALO), :] = high[...].astype(f32)
    grad_wide = unpack_rows(returned[...], slots_by(zrow[...], rows, 1, True))
    grad = grad_wide.astype(bf16)
    base = where_ref[0] * rows - HALO
    index = nb_t[...]
    index = jnp.where(index == scene, -1, index - base)
    span = rows + 2 * HALO
    sublanes = iota((span, rows), 0)
    wide = ker[...].astype(f32)
    total[...] = jnp.zeros_like(total)
    for k in range(nb_t.shape[0]):
        spread = dot(one_hot(index[k : k + 1, :] == sublanes), grad)
        total[...] += wide[k : k + 1, :] * spread
        kernel_grad[pl.ds(k, 1), :] = jnp.sum(extended[...] * spread, axis=0, keepdims=True)
    rim_low[...] = total[pl.ds(0, HALO), :]
    rim_high[...] = total[pl.ds(HALO + rows, HALO), :]
    centre[...] = total[pl.ds(HALO, rows), :] + grad_wide


def add_pieces(got, out):
    out[...] = jnp.sum(got[...].astype(f32), axis=0)


def unfold(where_ref, own, other, qkv_out, out_out, up_out, down_out, *, scale):
    core = where_ref[3]
    lower = jnp.where(core == 0, own[...], other[...]) * scale
    upper = jnp.where(core == 0, other[...], own[...]) * scale
    first = 0
    for result in (out_out, up_out):
        quarter = result.shape[1] // 4
        for place, half in enumerate((lower, upper)):
            for side in range(2):
                at = (2 * place + side) * quarter
                result[:, at : at + quarter] = half[4 * side : 4 * side + 4, first : first + quarter]
        first += quarter
    half_width = down_out.shape[1] // 2
    for place, half in enumerate((lower, upper)):
        for side in range(2):
            at = first + side * half_width
            down_out[8 * side : 8 * side + 8, place * half_width : (place + 1) * half_width] = half[
                :, at : at + half_width
            ]
    first += 2 * half_width
    quarter = qkv_out.shape[1] // 4
    for place, half in enumerate((lower, upper)):
        for side in range(2):
            at = (2 * place + side) * quarter
            qkv_out[:, at : at + quarter] = half[4 * side : 4 * side + 4, first : first + quarter]


def vmem():
    return pl.BlockSpec(memory_space=pltpu.VMEM)


def smem():
    return pl.BlockSpec(memory_space=pltpu.SMEM)


def shape(dims, dtype):
    return jax.ShapeDtypeStruct(dims, dtype)


def call(kernel, outs, inputs, scratch=(), limit=16, grid=None, in_specs=None, out_specs=None, name=None):
    return pl.pallas_call(
        kernel,
        out_shape=tuple(outs),
        in_specs=in_specs or [smem()] + [vmem()] * (len(inputs) - 1),
        out_specs=tuple(out_specs or [vmem()] * len(outs)),
        scratch_shapes=list(scratch),
        compiler_params=pltpu.CompilerParams(vmem_limit_bytes=limit * MB),
        name=name,
        **({} if grid is None else {"grid": grid}),
    )(*inputs)


def around(count, steps, stride=1):
    route = []
    for p in range(count):
        place = p // stride % GROUP
        route.append((p, p + ((place + steps) % GROUP - place) * stride))
    return route


def on_device(
    features, neighbours, z_to_hilbert, hilbert, conv_kernel, first_gain, second_gain,
    qkv_weight, out_weight, up_weight, down_weight, cotangent,
):
    points = features[0]
    rows, channels = points.shape
    devices = lax.axis_size("pts")
    device = lax.axis_index("pts")
    core = lax.axis_index("rep")
    replicas = lax.axis_size("rep")
    scene = rows * devices
    width = channels // GROUP
    hidden_width = up_weight.shape[1]
    offsets = neighbours.shape[2]
    patch = rows * GROUP
    group_heads = HEADS // GROUP
    where = jnp.stack([device, device % GROUP, device // GROUP % GROUP, core]).astype(jnp.int32)
    forward = [(i, i + 1) for i in range(devices - 1)]
    backward = [(i + 1, i) for i in range(devices - 1)]
    swap = [(0, 1), (1, 0)]
    low = lax.ppermute(points[rows - HALO :], "pts", forward)
    high = lax.ppermute(points[:HALO], "pts", backward)
    nb_t = neighbours[0].T
    gain1, gain2 = first_gain.reshape(1, channels), second_gain.reshape(1, channels)
    incoming = cotangent[0]

    (outgoing,) = call(
        functools.partial(conv_forward, scene=scene),
        [shape((4 * rows, channels // 2), bf16)],
        (where, low, points, high, nb_t, conv_kernel, z_to_hilbert),
        [pltpu.VMEM((rows + 2 * HALO, channels), bf16), pltpu.VMEM((rows, channels), bf16)],
        name="conv_forward",
    )

    def exchange(value):
        cut = value.reshape(devices, 2 * SLOTS, channels // 2)
        got = lax.all_to_all(cut, "pts", split_axis=0, concat_axis=0, tiled=True)
        return got.reshape(4 * rows, channels // 2)

    arrived = exchange(outgoing)

    ordered, shaped1, qkv = call(
        first_norm,
        [shape((rows, channels), bf16), shape((rows, channels), bf16), shape((GROUP, rows, 3 * width), bf16)],
        (where, arrived, hilbert, gain1, qkv_weight),
        name="first_norm",
    )

    def spread_out(blocks, stride=1):
        return [blocks[0]] + [lax.ppermute(blocks[j], "pts", around(devices, j, stride)) for j in range(1, GROUP)]

    def bring_back(blocks):
        return [blocks[0]] + [lax.ppermute(blocks[j], "pts", around(devices, -j)) for j in range(1, GROUP)]

    blocks = spread_out(qkv)

    by_head = pl.BlockSpec((1, patch, patch), lambda i: (i, 0, 0))
    probs, out_t, *attended = call(
        attention_forward,
        [shape((group_heads, patch, patch), bf16), shape((width, patch), f32)]
        + [shape((rows, width), bf16)] * GROUP,
        blocks,
        [
            pltpu.VMEM((patch, width), bf16),
            pltpu.VMEM((patch, width), bf16),
            pltpu.VMEM((width, patch), bf16),
            pltpu.SMEM((1,), f32),
        ],
        limit=24,
        grid=(group_heads,),
        in_specs=[vmem()] * GROUP,
        out_specs=[by_head] + [vmem()] * (1 + GROUP),
        name="attention_forward",
    )

    attended = bring_back(attended)

    chunk = hidden_width // 4
    kept_width = (2 * channels + hidden_width) // 2
    pack_width = 3 * channels + hidden_width + kept_width
    mixed_rows, grad_between, upstream, second_gain_part, pack, kept = call(
        mlp,
        [
            shape((rows, channels), bf16),
            shape((rows, channels), bf16),
            shape((GROUP, rows, width), bf16),
            shape((1, channels), f32),
            shape((rows, pack_width), bf16),
            shape((rows, kept_width), bf16),
        ],
        (where, *attended, ordered, shaped1, out_weight, gain2, incoming, up_weight, down_weight),
        [
            pltpu.VMEM((rows, channels), f32),
            pltpu.VMEM((rows, channels), bf16),
            pltpu.VMEM((rows, channels), f32),
            pltpu.VMEM((rows, 128), f32),
            pltpu.VMEM((rows, channels), f32),
            pltpu.VMEM((rows, channels), f32),
        ],
        limit=20,
        grid=(4,),
        in_specs=[smem()]
        + [vmem()] * (GROUP + 5)
        + [
            pl.BlockSpec((channels, chunk), lambda i: (0, i)),
            pl.BlockSpec((chunk, channels), lambda i: (i, 0)),
        ],
        name="mlp",
    )

    upper = spread_out(upstream)
    came = lax.ppermute(pack, "rep", swap)

    (early,) = call(
        functools.partial(early_products, channels=channels),
        [shape((GROUP, rows, 9 * channels // 4), bf16)],
        (where, pack, kept, came),
        limit=20,
        name="early_products",
    )
    early_parts = spread_out(early, GROUP)
    *upper, early_own = lax.optimization_barrier((*upper, early_parts[0]))

    grads = call(
        attention_backward,
        [shape((rows, 3 * width), bf16)] * GROUP,
        (*blocks, *upper, probs, out_t),
        [
            pltpu.VMEM((patch, width), bf16),
            pltpu.VMEM((patch, width), bf16),
            pltpu.VMEM((patch, width), bf16),
            pltpu.VMEM((patch, width), bf16),
            pltpu.VMEM((width, patch), bf16),
            pltpu.VMEM((width, patch), f32),
            pltpu.VMEM((width, patch), f32),
            pltpu.VMEM((patch, width), f32),
            pltpu.VMEM((patch, width), f32),
        ],
        limit=24,
        grid=(group_heads,),
        in_specs=[vmem()] * (2 * GROUP) + [by_head, vmem()],
        name="attention_backward",
    )

    grads = bring_back(grads)

    qkv_kept, qkv_sent, homeward, first_gain_part = call(
        qkv_backward,
        [
            shape((rows, 3 * channels // 2), bf16),
            shape((rows, 3 * channels // 2), bf16),
            shape((4 * rows, channels // 2), bf16),
            shape((1, channels), f32),
        ],
        (where, *grads, ordered, qkv_weight, gain1, grad_between, hilbert),
        [pltpu.VMEM((rows, 3 * channels), bf16)],
        name="qkv_backward",
    )

    returned = exchange(homeward)

    qkv_came = lax.ppermute(qkv_sent, "rep", swap)
    other_shaped1 = came[:, 2 * channels + hidden_width : 3 * channels + hidden_width]
    (late,) = call(
        functools.partial(late_products, channels=channels),
        [shape((GROUP, rows, 3 * channels // 4), bf16)],
        (where, shaped1, other_shaped1, qkv_kept, qkv_came),
        name="late_products",
    )
    late_parts = spread_out(late, GROUP)

    def total_of(parts):
        wide = [part.astype(f32) for part in parts]
        return ((wide[0] + wide[1]) + (wide[2] + wide[3])).astype(bf16)

    piece = jnp.concatenate([total_of([early_own] + early_parts[1:]), total_of(late_parts)], axis=1)
    returned, piece = lax.optimization_barrier((returned, piece))

    rim_low, rim_high, centre, kernel_part = call(
        functools.partial(conv_backward, scene=scene),
        [
            shape((HALO, channels), f32),
            shape((HALO, channels), f32),
            shape((rows, channels), f32),
            shape((offsets, channels), f32),
        ],
        (where, returned, low, points, high, nb_t, conv_kernel, z_to_hilbert),
        [pltpu.VMEM((rows + 2 * HALO, channels), f32), pltpu.VMEM((rows + 2 * HALO, channels), f32)],
        name="conv_backward",
    )

    from_above = lax.ppermute(rim_low, "pts", backward)
    from_below = lax.ppermute(rim_high, "pts", forward)
    centre = centre.at[:HALO].add(from_below).at[rows - HALO :].add(from_above)
    grad_features = centre.astype(bf16)

    layers = devices // (GROUP * GROUP)
    groups = [
        [z * GROUP * GROUP + y * GROUP + x for z in range(layers) for x in range(GROUP)] for y in range(GROUP)
    ]
    got = lax.all_to_all(
        piece.reshape(devices // GROUP, 8, 3 * channels),
        "pts", split_axis=0, concat_axis=0, axis_index_groups=groups, tiled=True,
    )
    (owned,) = call(
        add_pieces, [shape((8, 3 * channels), f32)], (got,), in_specs=[vmem()], name="add_pieces"
    )
    other = lax.ppermute(owned, "rep", swap)
    scale = 1.0 / math.sqrt(scene * replicas)
    weight_grads = call(
        functools.partial(unfold, scale=scale),
        [
            shape((4, 3 * channels), f32),
            shape((4, channels), f32),
            shape((4, hidden_width), f32),
            shape((down_weight.shape[0] // devices, channels), f32),
        ],
        (where, owned, other),
        name="unfold",
    )

    small = jnp.concatenate([kernel_part, first_gain_part, second_gain_part], axis=0)
    half = channels // 2
    sums = lax.dynamic_slice_in_dim(small, core * half, half, 1) + lax.ppermute(
        lax.dynamic_slice_in_dim(small, (1 - core) * half, half, 1), "rep", swap
    )
    for bit in range(log2(devices)):
        sums = sums + lax.ppermute(sums, "pts", [(p, p ^ (1 << bit)) for p in range(devices)])
    sums = sums * scale
    partner = lax.ppermute(sums, "rep", swap)
    small = jnp.concatenate([jnp.where(core == 0, sums, partner), jnp.where(core == 0, partner, sums)], axis=1)

    return (
        mixed_rows[None],
        grad_features[None],
        small[:offsets],
        small[offsets],
        small[offsets + 1],
        *weight_grads,
    )


def solution(mesh):
    return jax.shard_map(
        on_device,
        mesh=mesh,
        in_specs=(
            P("rep", "pts", None),
            P("rep", "pts", None),
            P("rep", "pts"),
            P("rep", "pts"),
            P(),
            P(),
            P(),
            P(),
            P(),
            P(),
            P(),
            P("rep", "pts", None),
        ),
        out_specs=(
            P("rep", "pts", None),
            P("rep", "pts", None),
            P(),
            P(),
            P(),
            P("pts", None),
            P("pts", None),
            P("pts", None),
            P("pts", None),
        ),
        check_vma=False,
    )
```

```python
import functools
import math

import jax
import jax.numpy as jnp
from jax import lax
from jax.experimental import pallas as pl
from jax.experimental.pallas import tpu as pltpu
from jax.sharding import PartitionSpec as P

HEADS = 32
GROUP = 4
HALO = 32
HEAD = 16
SLOTS = 4

epsilon = 1e-05
root_half = 0.7071067811865476
gauss_norm = 0.3989422804014327

f32 = jnp.float32
bf16 = jnp.bfloat16
MB = 1 << 20


def dot(left, right):
    return jnp.dot(left, right, preferred_element_type=f32)


def against(left, right):
    return lax.dot_general(left, right, (((1,), (1,)), ((), ())), preferred_element_type=f32)


def contract(left, right):
    return lax.dot_general(left, right, (((0,), (0,)), ((), ())), preferred_element_type=f32)


def iota(shape, dim):
    return lax.broadcasted_iota(jnp.int32, shape, dim)


def one_hot(condition):
    return jnp.where(condition, 1.0, 0.0).astype(bf16)


def normalize(widened):
    centre = jnp.mean(widened, axis=-1, keepdims=True)
    shifted = widened - centre
    scale = lax.rsqrt(jnp.mean(shifted * shifted, axis=-1, keepdims=True) + epsilon)
    return shifted * scale, scale


def norm_back(grad_shaped, normed, scale, gain):
    scaled = grad_shaped * gain
    centred = scaled - jnp.mean(scaled, axis=-1, keepdims=True)
    return scale * (centred - normed * jnp.mean(scaled * normed, axis=-1, keepdims=True))


def gelu_parts(hidden):
    normal_cdf = 0.5 * (1.0 + lax.erf(hidden * root_half))
    return (hidden * normal_cdf, normal_cdf + hidden * gauss_norm * jnp.exp(-0.5 * hidden * hidden))


def log2(number):
    return number.bit_length() - 1


def column(row):
    tall = jnp.broadcast_to(row.astype(f32), (128, row.shape[1]))
    return tall.T[:, :1].astype(jnp.int32)


def slots_by(row, rows, along, order):
    peer_row, col = row >> log2(rows), column(row)
    peer_col = col >> log2(rows)
    dims = (col.shape[0], row.shape[1])
    if order:
        before = iota(dims, 0) < iota(dims, 1) if along == 0 else iota(dims, 1) < iota(dims, 0)
    else:
        before = col < row if along == 0 else row < col
    rank = jnp.sum(jnp.where((peer_row == peer_col) & before, 1, 0), axis=along, keepdims=True)
    peer = peer_row if along == 0 else peer_col
    return peer * (2 * SLOTS) + rank


def pack_rows(values, slot):
    rows, channels = values.shape
    half = channels // 2
    stacked = jnp.concatenate([values[:, :half], values[:, half:]], axis=0)
    wanted = jnp.concatenate([slot, slot + SLOTS], axis=1)
    pick = one_hot(iota((4 * rows, 2 * rows), 0) == wanted)
    return dot(pick, stacked).astype(bf16)


def unpack_rows(packed, slot):
    lanes = iota((slot.shape[0], packed.shape[0]), 1)
    parts = [dot(one_hot(lanes == slot + half * SLOTS), packed) for half in range(2)]
    return jnp.concatenate(parts, axis=1)


def neighbour_rows(nb_t, base, far, scene):
    offsets, rows = nb_t.shape
    index = jnp.where(nb_t[...] == scene, far, nb_t[...] - base).astype(f32)
    index = jnp.concatenate([index, jnp.zeros((32 - offsets, rows), f32)], axis=0)
    return index.T.astype(jnp.int32)


def conv_inside(where_ref, own, nb_t, ker, out, total, *, scene):
    rows, channels = own.shape
    offsets = nb_t.shape[0]
    index = neighbour_rows(nb_t, where_ref[0] * rows, -(4 * rows), scene)
    wide = ker[...].astype(f32)
    half = rows // 2
    span = half + HALO
    lanes = iota((half, span), 1)
    for part in range(2):
        start = part * (rows - span)
        window = own[pl.ds(start, span), :]
        near = index[half * part : half * (part + 1), :] - start
        value = own[pl.ds(half * part, half), :].astype(f32)
        for k in range(offsets):
            value = value + wide[k : k + 1, :] * dot(one_hot(near[:, k : k + 1] == lanes), window)
        total[pl.ds(half * part, half), :] = value
    out[...] = total[...]


def conv_rims(where_ref, low, high, inside, nb_t, ker, zrow, out, halo, merged, *, scene):
    rows, channels = inside.shape
    offsets = nb_t.shape[0]
    halo[pl.ds(0, HALO), :] = low[...]
    halo[pl.ds(HALO, HALO), :] = high[...]
    index = neighbour_rows(nb_t, where_ref[0] * rows, -(4 * rows), scene)
    below, above = index[:HALO, :], index[rows - HALO :, :]
    below = jnp.where(below < 0, below + HALO, -1)
    above = jnp.where(above >= rows, above - rows + HALO, -1)
    near = jnp.concatenate([below, above], axis=0)
    wide = ker[...].astype(f32)
    lanes = iota((2 * HALO, 2 * HALO), 1)
    value = jnp.concatenate([inside[pl.ds(0, HALO), :], inside[pl.ds(rows - HALO, HALO), :]], axis=0)
    for k in range(offsets):
        value = value + wide[k : k + 1, :] * dot(one_hot(near[:, k : k + 1] == lanes), halo[...])
    merged[...] = inside[...].astype(bf16)
    merged[pl.ds(0, HALO), :] = value[:HALO].astype(bf16)
    merged[pl.ds(rows - HALO, HALO), :] = value[HALO:].astype(bf16)
    out[...] = pack_rows(merged[...], slots_by(zrow[...], rows, 0, True))


def first_norm(where_ref, arrived, hrow, gain, weight, ordered, shaped_out, qkv):
    rows, channels = ordered.shape
    points = unpack_rows(arrived[...], slots_by(hrow[...], rows, 1, False))
    ordered[...] = points.astype(bf16)
    normed, _ = normalize(points)
    shaped = (normed * gain[...]).astype(bf16)
    shaped_out[...] = shaped
    result = dot(shaped, weight[...]).astype(bf16)
    here = where_ref[1]
    width = channels // GROUP
    for group in range(GROUP):
        place = lax.rem(group - here + GROUP, GROUP)
        for kind in range(3):
            first = kind * channels + group * width
            qkv[place, :, kind * width : (kind + 1) * width] = result[:, first : first + width]


def attention_forward(b0, b1, b2, b3, probs, out_t, a0, a1, a2, a3, q_all, k_all, v_t, bound):
    head = pl.program_id(0)
    blocks = (b0, b1, b2, b3)
    rows = b0.shape[0]
    width = b0.shape[1] // 3
    keys = rows * GROUP
    factor = HEAD ** (-0.5)

    @pl.when(head == 0)
    def _():
        for place, block in enumerate(blocks):
            here = pl.ds(place * rows, rows)
            q_all[here, :] = (block[:, :width].astype(f32) * factor).astype(bf16)
            k_all[here, :] = block[:, width : 2 * width]
            v_t[:, place * rows : (place + 1) * rows] = block[:, 2 * width :].astype(f32).T.astype(bf16)
        groups = one_hot(iota((width, width), 0) // HEAD == iota((width, width), 1))
        lengths = []
        for ref in (q_all, k_all):
            wide = ref[...].astype(f32)
            lengths.append(jnp.max(dot((wide * wide).astype(bf16), groups), axis=0, keepdims=True))
        bound[0] = jnp.max(lengths[0] * lengths[1])

    mine = (iota((keys, width), 1) // HEAD) == head
    k_head = jnp.where(mine, k_all[...], jnp.zeros((), bf16))
    at = pl.multiple_of(head * HEAD, HEAD)
    v_head = v_t[pl.ds(at, HEAD), :]

    def softmax(shifted, parts):
        for part in range(parts):
            cols = slice(part * (keys // parts), (part + 1) * (keys // parts))
            scores = against(k_head, q_all[cols, :])
            if shifted:
                scores = scores - jnp.max(scores, axis=0, keepdims=True)
            exponent = jnp.exp(scores)
            inverse = 1.0 / jnp.sum(exponent, axis=0, keepdims=True)
            chance = (exponent * inverse).astype(bf16)
            probs[0, :, cols] = chance
            out_t[pl.ds(at, HEAD), cols] = dot(v_head, chance)

    calm = bound[0] <= 1500.0

    @pl.when(calm)
    def _():
        softmax(False, 1)

    @pl.when(jnp.logical_not(calm))
    def _():
        softmax(True, 4)

    @pl.when(head == pl.num_programs(0) - 1)
    def _():
        for place, result in enumerate((a0, a1, a2, a3)):
            result[...] = out_t[:, place * rows : (place + 1) * rows].T.astype(bf16)


def attention_backward(
    b0, b1, b2, b3, u0, u1, u2, u3, probs, out_t, g0, g1, g2, g3,
    q_all, k_all, v_all, u_all, k_t, spread_t, dq_t, dk, dv,
):
    head = pl.program_id(0)
    blocks = (b0, b1, b2, b3)
    rows = b0.shape[0]
    width = b0.shape[1] // 3
    keys = rows * GROUP
    factor = HEAD ** (-0.5)

    @pl.when(head == 0)
    def _():
        for place, (block, up) in enumerate(zip(blocks, (u0, u1, u2, u3))):
            here = pl.ds(place * rows, rows)
            cols = slice(place * rows, (place + 1) * rows)
            q_all[here, :] = block[:, :width]
            k_all[here, :] = block[:, width : 2 * width]
            v_all[here, :] = (block[:, 2 * width :].astype(f32) * factor).astype(bf16)
            u_all[here, :] = up[...]
            k_t[:, cols] = block[:, width : 2 * width].astype(f32).T.astype(bf16)
            spread_t[:, cols] = up[...].astype(f32).T * out_t[:, cols] * factor
        dk[...] = jnp.zeros_like(dk)
        dv[...] = jnp.zeros_like(dv)

    mine = (iota((keys, width), 1) // HEAD) == head
    nought = jnp.zeros((), bf16)
    v_head = jnp.where(mine, v_all[...], nought)
    at = pl.multiple_of(head * HEAD, HEAD)
    k_head = k_t[pl.ds(at, HEAD), :]
    for part in range(GROUP):
        cols = slice(part * rows, (part + 1) * rows)
        chance = probs[0, :, cols]
        grad = against(v_head, u_all[cols, :])
        spread = jnp.sum(spread_t[pl.ds(at, HEAD), cols], axis=0, keepdims=True)
        grad_scores = (chance.astype(f32) * (grad - spread)).astype(bf16)
        own = mine[:rows, :]
        dv[...] += dot(chance, jnp.where(own, u_all[cols, :], nought))
        dk[...] += dot(grad_scores, jnp.where(own, q_all[cols, :], nought))
        dq_t[pl.ds(at, HEAD), cols] = dot(k_head, grad_scores)

    @pl.when(head == pl.num_programs(0) - 1)
    def _():
        for place, result in enumerate((g0, g1, g2, g3)):
            here = pl.ds(place * rows, rows)
            result[:, :width] = dq_t[:, place * rows : (place + 1) * rows].T.astype(bf16)
            result[:, width : 2 * width] = dk[here, :].astype(bf16)
            result[:, 2 * width :] = dv[here, :].astype(bf16)


def mlp(
    where_ref, a0, a1, a2, a3, ordered, first_shaped, out_w, gain, cot, up, down,
    mixed, grad_between, upstream, gain_grad, pack, kept,
    between, shaped, normed, scale, sum_mixed, sum_grad,
):
    step = pl.program_id(0)
    rows, channels = ordered.shape
    width = channels // GROUP
    here, core = where_ref[1], where_ref[3]
    chunk = up.shape[1]
    hidden_width = chunk * 4
    right = 3 * channels + hidden_width

    @pl.when(step == 0)
    def _():
        for place, block in enumerate((a0, a1, a2, a3)):
            group = lax.rem(here + place, GROUP)
            pack[:, pl.ds(pl.multiple_of(group * width, width), width)] = block[...]
        attended = pack[:, :channels]
        total = (ordered[...].astype(f32) + dot(attended, out_w[...])).astype(bf16).astype(f32)
        between[...] = total
        normed_value, scale_value = normalize(total)
        normed[...] = normed_value
        scale[...] = jnp.broadcast_to(scale_value, scale.shape)
        shaped_value = (normed_value * gain[...]).astype(bf16)
        shaped[...] = shaped_value
        pack[:, channels : 2 * channels] = shaped_value
        pack[:, 2 * channels + hidden_width : right] = first_shaped[...]
        sum_mixed[...] = total
        sum_grad[...] = jnp.zeros_like(sum_grad)
        half = channels // 2
        at = right + (channels + hidden_width) // 2
        kept[:, (channels + hidden_width) // 2 :] = cot[:, pl.ds(pl.multiple_of(core * half, half), half)]
        pack[:, at:] = cot[:, pl.ds(pl.multiple_of((1 - core) * half, half), half)]

    hidden = dot(shaped[...], up[...])
    activation, derivative = gelu_parts(hidden)
    active = activation.astype(bf16)
    pack[:, pl.ds(pl.multiple_of(2 * channels + step * chunk, chunk), chunk)] = active
    sum_mixed[...] += dot(active, down[...])
    back = (against(cot[...], down[...]) * derivative).astype(bf16)
    sum_grad[...] += against(back, up[...])
    place = channels // 2 + lax.rem(step, 2) * chunk
    owner = step // 2

    @pl.when(owner == core)
    def _():
        kept[:, pl.ds(pl.multiple_of(place, 128), chunk)] = back

    @pl.when(owner != core)
    def _():
        pack[:, pl.ds(pl.multiple_of(right + place, 128), chunk)] = back

    @pl.when(step == pl.num_programs(0) - 1)
    def _():
        mixed[...] = sum_mixed[...].astype(bf16)
        grad_second = sum_grad[...]
        gain_grad[...] = jnp.sum(grad_second * normed[...], axis=0, keepdims=True)
        grad = norm_back(grad_second, normed[...], scale[:, :1], gain[...]) + cot[...].astype(f32)
        grad = grad.astype(bf16)
        grad_between[...] = grad
        half = channels // 2
        kept[:, :half] = grad_between[:, pl.ds(pl.multiple_of(core * half, half), half)]
        pack[:, right : right + half] = grad_between[:, pl.ds(pl.multiple_of((1 - core) * half, half), half)]
        result = against(grad, out_w[...]).astype(bf16)
        for group in range(GROUP):
            place = lax.rem(group - here + GROUP, GROUP)
            upstream[place, :, :] = result[:, group * width : (group + 1) * width]


def qkv_backward(
    where_ref, g0, g1, g2, g3, ordered, weight, gain, grad_between, hrow,
    kept, sent, homeward, gain_grad, grad_qkv,
):
    rows, channels = ordered.shape
    width = channels // GROUP
    here, core = where_ref[1], where_ref[3]
    for place, block in enumerate((g0, g1, g2, g3)):
        group = lax.rem(here + place, GROUP)
        for kind in range(3):
            first = pl.multiple_of(kind * channels + group * width, width)
            grad_qkv[:, pl.ds(first, width)] = block[:, kind * width : (kind + 1) * width]
    grad_first = against(grad_qkv[...], weight[...])
    normed, scale = normalize(ordered[...].astype(f32))
    gain_grad[...] = jnp.sum(grad_first * normed, axis=0, keepdims=True)
    grad = norm_back(grad_first, normed, scale, gain[...]) + grad_between[...].astype(f32)
    homeward[...] = pack_rows(grad.astype(bf16), slots_by(hrow[...], rows, 0, False))
    half = 3 * channels // 2
    kept[...] = grad_qkv[:, pl.ds(pl.multiple_of(core * half, 128), half)]
    sent[...] = grad_qkv[:, pl.ds(pl.multiple_of((1 - core) * half, 128), half)]


def fold_rows(product):
    rows, columns = product.shape
    half = columns // 2
    tiles = product.reshape(rows // 8, 8, columns)
    turned = pltpu.roll(tiles, 4, 1)
    above = iota((rows // 8, 8, half), 1) < 4
    even = jnp.where(above, tiles[:, :, :half], turned[:, :, half:])
    odd = jnp.where(above, turned[:, :, :half], tiles[:, :, half:])
    return even, odd


def place_folded(out, folded, first, chunk):
    even, odd = folded
    span = even.shape[2]
    for level in range(2):
        for y in range(GROUP):
            q = level * 8 + y * 2
            tall = jnp.concatenate([even[q], odd[q], even[q + 1], odd[q + 1]], axis=0)
            at = (2 * chunk + level) * 32
            out[y, at : at + 32, first : first + span] = tall.astype(bf16)


def hand_out(pieces, here, own, up, down, far_up, far_down):
    half = far_up.shape[0]
    own[...] = pieces[here]
    up[...] = pieces[lax.rem(here + 1, GROUP)]
    down[...] = pieces[lax.rem(here + 3, GROUP)]
    far = lax.rem(here + 2, GROUP)
    far_up[...] = pieces[far, :half, :]
    far_down[...] = pieces[far, half:, :]


def relay(up, down, from_below, from_above, out_up, out_down):
    half = from_below.shape[0]
    out_up[:half, :] = (up[:half, :].astype(f32) + from_below[...].astype(f32)).astype(bf16)
    out_up[half:, :] = up[half:, :]
    out_down[:half, :] = down[:half, :]
    out_down[half:, :] = (down[half:, :].astype(f32) + from_above[...].astype(f32)).astype(bf16)


def early_products(where_ref, pack, kept, came, own, up, down, far_up, far_down, out, *, channels):
    here = where_ref[2]
    hidden_width = pack.shape[1] - kept.shape[1] - 3 * channels
    right = 3 * channels + hidden_width
    half_out, half_up = channels // 2, hidden_width // 2

    def product(left, first, span):
        return contract(pack[:, left], kept[:, first : first + span]) + contract(
            came[:, left], came[:, right + first : right + first + span]
        )

    for chunk in range(4):
        at = chunk * 128
        part = product(slice(at, at + 128), 0, half_out)
        place_folded(out, fold_rows(part), 0, chunk)
        part = product(slice(channels + at, channels + at + 128), half_out, half_up)
        place_folded(out, fold_rows(part), half_out // 2, chunk)
        at = 2 * channels + chunk * 512
        part = product(slice(at, at + 512), half_out + half_up, half_out)
        tiles = part.reshape(32, 2, 8, half_out)
        first = (half_out + half_up) // 2
        for level in range(2):
            for y in range(GROUP):
                q = level * 16 + y * 4
                row = (2 * chunk + level) * 32
                for side in range(2):
                    flat = tiles[q : q + 4, side].reshape(32, half_out).astype(bf16)
                    out[y, row : row + 32, first + side * half_out : first + (side + 1) * half_out] = flat
    hand_out(out, here, own, up, down, far_up, far_down)


def late_products(where_ref, pack, came_pack, kept, came, own, up, down, far_up, far_down, out, *, channels):
    here = where_ref[2]
    for chunk in range(4):
        at = slice(chunk * 128, chunk * 128 + 128)
        part = contract(pack[:, at], kept[...]) + contract(came_pack[:, at], came[...])
        place_folded(out, fold_rows(part), 0, chunk)
    hand_out(out, here, own, up, down, far_up, far_down)


def conv_backward(
    where_ref, returned, low, own, high, nb_t, ker, zrow, first_part, second_part,
    rim_low, rim_high, centre, small, extended, total, *, scene,
):
    rows, channels = own.shape
    offsets = nb_t.shape[0]
    extended[pl.ds(0, HALO), :] = low[...].astype(f32)
    extended[pl.ds(HALO, rows), :] = own[...].astype(f32)
    extended[pl.ds(HALO + rows, HALO), :] = high[...].astype(f32)
    grad_wide = unpack_rows(returned[...], slots_by(zrow[...], rows, 1, True))
    grad = grad_wide.astype(bf16)
    base = where_ref[0] * rows - HALO
    index = nb_t[...]
    index = jnp.where(index == scene, -1, index - base)
    span = rows + 2 * HALO
    sublanes = iota((span, rows), 0)
    wide = ker[...].astype(f32)
    total[...] = jnp.zeros_like(total)
    for k in range(offsets):
        spread = dot(one_hot(index[k : k + 1, :] == sublanes), grad)
        total[...] += wide[k : k + 1, :] * spread
        small[pl.ds(k, 1), :] = jnp.sum(extended[...] * spread, axis=0, keepdims=True)
    small[pl.ds(offsets, 1), :] = first_part[...]
    small[pl.ds(offsets + 1, 1), :] = second_part[...]
    rim_low[...] = total[pl.ds(0, HALO), :]
    rim_high[...] = total[pl.ds(HALO + rows, HALO), :]
    centre[...] = total[pl.ds(HALO, rows), :] + grad_wide


def early_total(e0, e1, e2, out):
    out[...] = (e0[...].astype(f32) + (e1[...].astype(f32) + e2[...].astype(f32))).astype(bf16)


def ring_total(early, l0, l1, l2, out):
    span = early.shape[1]
    out[:, :span] = early[...]
    out[:, span:] = (l0[...].astype(f32) + (l1[...].astype(f32) + l2[...].astype(f32))).astype(bf16)


def add_pieces(got, out):
    out[...] = jnp.sum(got[...].astype(f32), axis=0)


def unfold(where_ref, own, other, qkv_out, out_out, up_out, down_out, *, scale):
    core = where_ref[3]
    lower = jnp.where(core == 0, own[...], other[...]) * scale
    upper = jnp.where(core == 0, other[...], own[...]) * scale
    first = 0
    for result in (out_out, up_out):
        quarter = result.shape[1] // 4
        for place, half in enumerate((lower, upper)):
            for side in range(2):
                at = (2 * place + side) * quarter
                result[:, at : at + quarter] = half[4 * side : 4 * side + 4, first : first + quarter]
        first += quarter
    half_width = down_out.shape[1] // 2
    for place, half in enumerate((lower, upper)):
        for side in range(2):
            at = first + side * half_width
            down_out[8 * side : 8 * side + 8, place * half_width : (place + 1) * half_width] = half[
                :, at : at + half_width
            ]
    first += 2 * half_width
    quarter = qkv_out.shape[1] // 4
    for place, half in enumerate((lower, upper)):
        for side in range(2):
            at = (2 * place + side) * quarter
            qkv_out[:, at : at + quarter] = half[4 * side : 4 * side + 4, first : first + quarter]


def vmem():
    return pl.BlockSpec(memory_space=pltpu.VMEM)


def smem():
    return pl.BlockSpec(memory_space=pltpu.SMEM)


def shape(dims, dtype):
    return jax.ShapeDtypeStruct(dims, dtype)


def call(kernel, outs, inputs, scratch=(), limit=16, grid=None, in_specs=None, out_specs=None, name=None):
    return pl.pallas_call(
        kernel,
        out_shape=tuple(outs),
        in_specs=in_specs or [smem()] + [vmem()] * (len(inputs) - 1),
        out_specs=tuple(out_specs or [vmem()] * len(outs)),
        scratch_shapes=list(scratch),
        compiler_params=pltpu.CompilerParams(vmem_limit_bytes=limit * MB),
        name=name,
        **({} if grid is None else {"grid": grid}),
    )(*inputs)


def around(count, steps, stride=1):
    route = []
    for p in range(count):
        place = p // stride % GROUP
        route.append((p, p + ((place + steps) % GROUP - place) * stride))
    return route


def on_device(
    features, neighbours, z_to_hilbert, hilbert, conv_kernel, first_gain, second_gain,
    qkv_weight, out_weight, up_weight, down_weight, cotangent,
):
    points = features[0]
    rows, channels = points.shape
    devices = lax.axis_size("pts")
    device = lax.axis_index("pts")
    core = lax.axis_index("rep")
    replicas = lax.axis_size("rep")
    scene = rows * devices
    width = channels // GROUP
    hidden_width = up_weight.shape[1]
    offsets = neighbours.shape[2]
    patch = rows * GROUP
    group_heads = HEADS // GROUP
    where = jnp.stack([device, device % GROUP, device // GROUP % GROUP, core]).astype(jnp.int32)
    forward = [(i, i + 1) for i in range(devices - 1)]
    backward = [(i + 1, i) for i in range(devices - 1)]
    swap = [(0, 1), (1, 0)]
    low = lax.ppermute(points[rows - HALO :], "pts", forward)
    high = lax.ppermute(points[:HALO], "pts", backward)
    nb_t = neighbours[0].T
    gain1, gain2 = first_gain.reshape(1, channels), second_gain.reshape(1, channels)
    incoming = cotangent[0]

    (inside,) = call(
        functools.partial(conv_inside, scene=scene),
        [shape((rows, channels), f32)],
        (where, points, nb_t, conv_kernel),
        [pltpu.VMEM((rows, channels), f32)],
        name="conv_inside",
    )
    (outgoing,) = call(
        functools.partial(conv_rims, scene=scene),
        [shape((4 * rows, channels // 2), bf16)],
        (where, low, high, inside, nb_t, conv_kernel, z_to_hilbert),
        [pltpu.VMEM((2 * HALO, channels), bf16), pltpu.VMEM((rows, channels), bf16)],
        name="conv_rims",
    )

    def exchange(value):
        cut = value.reshape(devices, 2 * SLOTS, channels // 2)
        got = lax.all_to_all(cut, "pts", split_axis=0, concat_axis=0, tiled=True)
        return got.reshape(4 * rows, channels // 2)

    arrived = exchange(outgoing)

    ordered, shaped1, qkv = call(
        first_norm,
        [shape((rows, channels), bf16), shape((rows, channels), bf16), shape((GROUP, rows, 3 * width), bf16)],
        (where, arrived, hilbert, gain1, qkv_weight),
        name="first_norm",
    )

    def spread_out(blocks, stride=1):
        return [blocks[0]] + [lax.ppermute(blocks[j], "pts", around(devices, j, stride)) for j in range(1, GROUP)]

    def bring_back(blocks):
        return [blocks[0]] + [lax.ppermute(blocks[j], "pts", around(devices, -j)) for j in range(1, GROUP)]

    blocks = spread_out(qkv)

    by_head = pl.BlockSpec((1, patch, patch), lambda i: (i, 0, 0))
    probs, out_t, *attended = call(
        attention_forward,
        [shape((group_heads, patch, patch), bf16), shape((width, patch), f32)]
        + [shape((rows, width), bf16)] * GROUP,
        blocks,
        [
            pltpu.VMEM((patch, width), bf16),
            pltpu.VMEM((patch, width), bf16),
            pltpu.VMEM((width, patch), bf16),
            pltpu.SMEM((1,), f32),
        ],
        limit=24,
        grid=(group_heads,),
        in_specs=[vmem()] * GROUP,
        out_specs=[by_head] + [vmem()] * (1 + GROUP),
        name="attention_forward",
    )

    attended = bring_back(attended)

    chunk = hidden_width // 4
    kept_width = (2 * channels + hidden_width) // 2
    pack_width = 3 * channels + hidden_width + kept_width
    mixed_rows, grad_between, upstream, second_gain_part, pack, kept = call(
        mlp,
        [
            shape((rows, channels), bf16),
            shape((rows, channels), bf16),
            shape((GROUP, rows, width), bf16),
            shape((1, channels), f32),
            shape((rows, pack_width), bf16),
            shape((rows, kept_width), bf16),
        ],
        (where, *attended, ordered, shaped1, out_weight, gain2, incoming, up_weight, down_weight),
        [
            pltpu.VMEM((rows, channels), f32),
            pltpu.VMEM((rows, channels), bf16),
            pltpu.VMEM((rows, channels), f32),
            pltpu.VMEM((rows, 128), f32),
            pltpu.VMEM((rows, channels), f32),
            pltpu.VMEM((rows, channels), f32),
        ],
        limit=20,
        grid=(4,),
        in_specs=[smem()]
        + [vmem()] * (GROUP + 5)
        + [
            pl.BlockSpec((channels, chunk), lambda i: (0, i)),
            pl.BlockSpec((chunk, channels), lambda i: (i, 0)),
        ],
        name="mlp",
    )

    upper = spread_out(upstream)
    came = lax.ppermute(pack, "rep", swap)
    *upper, came = lax.optimization_barrier((*upper, came))

    def ring_shapes(columns):
        full, half = shape((rows, columns), bf16), shape((rows // 2, columns), bf16)
        return [full, full, full, half, half]

    def step(value, steps):
        return lax.ppermute(value, "pts", around(devices, steps, GROUP))

    def relayed(up, down, below, above):
        return call(
            relay, [shape(up.shape, bf16)] * 2, (up, down, below, above), in_specs=[vmem()] * 4, name="relay"
        )

    columns = 9 * channels // 4
    early_own, up, down, far_up, far_down = call(
        functools.partial(early_products, channels=channels),
        ring_shapes(columns),
        (where, pack, kept, came),
        [pltpu.VMEM((GROUP, rows, columns), bf16)],
        limit=20,
        name="early_products",
    )
    below, above = step(far_up, 1), step(far_down, -1)
    *upper, early_own = lax.optimization_barrier((*upper, early_own))

    grads = call(
        attention_backward,
        [shape((rows, 3 * width), bf16)] * GROUP,
        (*blocks, *upper, probs, out_t),
        [
            pltpu.VMEM((patch, width), bf16),
            pltpu.VMEM((patch, width), bf16),
            pltpu.VMEM((patch, width), bf16),
            pltpu.VMEM((patch, width), bf16),
            pltpu.VMEM((width, patch), bf16),
            pltpu.VMEM((width, patch), f32),
            pltpu.VMEM((width, patch), f32),
            pltpu.VMEM((patch, width), f32),
            pltpu.VMEM((patch, width), f32),
        ],
        limit=24,
        grid=(group_heads,),
        in_specs=[vmem()] * (2 * GROUP) + [by_head, vmem()],
        name="attention_backward",
    )

    *grads, below, above = lax.optimization_barrier((*grads, below, above))
    grads = bring_back(grads)
    up, down = relayed(up, down, below, above)
    below, above = step(up, 1), step(down, -1)
    *grads, below, above = lax.optimization_barrier((*grads, below, above))
    qkv_kept, qkv_sent, homeward, first_gain_part = call(
        qkv_backward,
        [
            shape((rows, 3 * channels // 2), bf16),
            shape((rows, 3 * channels // 2), bf16),
            shape((4 * rows, channels // 2), bf16),
            shape((1, channels), f32),
        ],
        (where, *grads, ordered, qkv_weight, gain1, grad_between, hilbert),
        [pltpu.VMEM((rows, 3 * channels), bf16)],
        name="qkv_backward",
    )

    returned = exchange(homeward)
    (early,) = call(
        early_total, [shape(early_own.shape, bf16)], (early_own, below, above), in_specs=[vmem()] * 3,
        name="early_total",
    )
    returned, early = lax.optimization_barrier((returned, early))
    qkv_came = lax.ppermute(qkv_sent, "rep", swap)
    other_shaped1 = came[:, 2 * channels + hidden_width : 3 * channels + hidden_width]
    columns = 3 * channels // 4
    late_own, up, down, far_up, far_down = call(
        functools.partial(late_products, channels=channels),
        ring_shapes(columns),
        (where, shaped1, other_shaped1, qkv_kept, qkv_came),
        [pltpu.VMEM((GROUP, rows, columns), bf16)],
        name="late_products",
    )
    up, down = relayed(up, down, step(far_up, 1), step(far_down, -1))
    late_parts = (late_own, step(up, 1), step(down, -1))

    rim_low, rim_high, centre, small = call(
        functools.partial(conv_backward, scene=scene),
        [
            shape((HALO, channels), f32),
            shape((HALO, channels), f32),
            shape((rows, channels), f32),
            shape((offsets + 2, channels), f32),
        ],
        (
            where, returned, low, points, high, nb_t, conv_kernel, z_to_hilbert,
            first_gain_part, second_gain_part,
        ),
        [pltpu.VMEM((rows + 2 * HALO, channels), f32), pltpu.VMEM((rows + 2 * HALO, channels), f32)],
        name="conv_backward",
    )

    from_above = lax.ppermute(rim_low, "pts", backward)
    from_below = lax.ppermute(rim_high, "pts", forward)
    centre = centre.at[:HALO].add(from_below).at[rows - HALO :].add(from_above)
    grad_features = centre.astype(bf16)

    _, *late_parts = lax.optimization_barrier((small, *late_parts))
    (piece,) = call(
        ring_total, [shape((rows, 3 * channels), bf16)], (early, *late_parts),
        in_specs=[vmem()] * 4, name="ring_total",
    )
    layers = devices // (GROUP * GROUP)
    groups = [
        [z * GROUP * GROUP + y * GROUP + x for z in range(layers) for x in range(GROUP)] for y in range(GROUP)
    ]
    got = lax.all_to_all(
        piece.reshape(devices // GROUP, 8, 3 * channels),
        "pts", split_axis=0, concat_axis=0, axis_index_groups=groups, tiled=True,
    )
    (owned,) = call(
        add_pieces, [shape((8, 3 * channels), f32)], (got,), in_specs=[vmem()], name="add_pieces"
    )
    other = lax.ppermute(owned, "rep", swap)
    scale = 1.0 / math.sqrt(scene * replicas)
    weight_grads = call(
        functools.partial(unfold, scale=scale),
        [
            shape((4, 3 * channels), f32),
            shape((4, channels), f32),
            shape((4, hidden_width), f32),
            shape((down_weight.shape[0] // devices, channels), f32),
        ],
        (where, owned, other),
        name="unfold",
    )

    def partner(value, axis, mask):
        count = replicas if axis == "rep" else devices
        return lax.ppermute(value, axis, [(p, p ^ mask) for p in range(count)])

    bit = 1
    while bit < devices:
        if 4 * bit <= devices:
            near, far, across = [partner(small, "pts", m * bit) for m in (1, 2, 3)]
            small = (small + near) + (far + across)
            bit *= 4
        else:
            small = small + partner(small, "pts", bit)
            bit *= 2
    small = (small + partner(small, "rep", 1)) * scale

    return (
        mixed_rows[None],
        grad_features[None],
        small[:offsets],
        small[offsets],
        small[offsets + 1],
        *weight_grads,
    )


def solution(mesh):
    return jax.shard_map(
        on_device,
        mesh=mesh,
        in_specs=(
            P("rep", "pts", None),
            P("rep", "pts", None),
            P("rep", "pts"),
            P("rep", "pts"),
            P(),
            P(),
            P(),
            P(),
            P(),
            P(),
            P(),
            P("rep", "pts", None),
        ),
        out_specs=(
            P("rep", "pts", None),
            P("rep", "pts", None),
            P(),
            P(),
            P(),
            P("pts", None),
            P("pts", None),
            P("pts", None),
            P("pts", None),
        ),
        check_vma=False,
    )
```

```python
import functools
import math

import jax
import jax.numpy as jnp
from jax import lax
from jax.experimental import pallas as pl
from jax.experimental.pallas import tpu as pltpu
from jax.sharding import PartitionSpec as P

HEADS = 32
GROUP = 4
HALO = 32
HEAD = 16
SLOTS = 4

epsilon = 1e-05
root_half = 0.7071067811865476
gauss_norm = 0.3989422804014327

f32 = jnp.float32
bf16 = jnp.bfloat16
MB = 1 << 20


def dot(left, right):
    return jnp.dot(left, right, preferred_element_type=f32)


def against(left, right):
    return lax.dot_general(left, right, (((1,), (1,)), ((), ())), preferred_element_type=f32)


def contract(left, right):
    return lax.dot_general(left, right, (((0,), (0,)), ((), ())), preferred_element_type=f32)


def iota(shape, dim):
    return lax.broadcasted_iota(jnp.int32, shape, dim)


def one_hot(condition):
    return jnp.where(condition, 1.0, 0.0).astype(bf16)


def normalize(widened):
    centre = jnp.mean(widened, axis=-1, keepdims=True)
    shifted = widened - centre
    scale = lax.rsqrt(jnp.mean(shifted * shifted, axis=-1, keepdims=True) + epsilon)
    return shifted * scale, scale


def norm_back(grad_shaped, normed, scale, gain):
    scaled = grad_shaped * gain
    centred = scaled - jnp.mean(scaled, axis=-1, keepdims=True)
    return scale * (centred - normed * jnp.mean(scaled * normed, axis=-1, keepdims=True))


def gelu_parts(hidden):
    normal_cdf = 0.5 * (1.0 + lax.erf(hidden * root_half))
    return (hidden * normal_cdf, normal_cdf + hidden * gauss_norm * jnp.exp(-0.5 * hidden * hidden))


def log2(number):
    return number.bit_length() - 1


def column(row):
    tall = jnp.broadcast_to(row.astype(f32), (128, row.shape[1]))
    return tall.T[:, :1].astype(jnp.int32)


def slots_by(row, rows, along, order):
    peer_row, col = row >> log2(rows), column(row)
    peer_col = col >> log2(rows)
    dims = (col.shape[0], row.shape[1])
    if order:
        before = iota(dims, 0) < iota(dims, 1) if along == 0 else iota(dims, 1) < iota(dims, 0)
    else:
        before = col < row if along == 0 else row < col
    rank = jnp.sum(jnp.where((peer_row == peer_col) & before, 1, 0), axis=along, keepdims=True)
    peer = peer_row if along == 0 else peer_col
    return peer * (2 * SLOTS) + rank


def pack_rows(values, slot):
    rows, channels = values.shape
    half = channels // 2
    stacked = jnp.concatenate([values[:, :half], values[:, half:]], axis=0)
    wanted = jnp.concatenate([slot, slot + SLOTS], axis=1)
    pick = one_hot(iota((4 * rows, 2 * rows), 0) == wanted)
    return dot(pick, stacked).astype(bf16)


def unpack_rows(packed, slot):
    lanes = iota((slot.shape[0], packed.shape[0]), 1)
    parts = [dot(one_hot(lanes == slot + half * SLOTS), packed) for half in range(2)]
    return jnp.concatenate(parts, axis=1)


def neighbour_rows(nb_t, base, far, scene):
    offsets, rows = nb_t.shape
    index = jnp.where(nb_t[...] == scene, far, nb_t[...] - base).astype(f32)
    index = jnp.concatenate([index, jnp.zeros((32 - offsets, rows), f32)], axis=0)
    return index.T.astype(jnp.int32)


def conv_inside(where_ref, own, nb_t, ker, out, total, *, scene):
    rows, channels = own.shape
    offsets = nb_t.shape[0]
    index = neighbour_rows(nb_t, where_ref[0] * rows, -(4 * rows), scene)
    wide = ker[...].astype(f32)
    half = rows // 2
    span = half + HALO
    lanes = iota((half, span), 1)
    for part in range(2):
        start = part * (rows - span)
        window = own[pl.ds(start, span), :]
        near = index[half * part : half * (part + 1), :] - start
        value = own[pl.ds(half * part, half), :].astype(f32)
        for k in range(offsets):
            value = value + wide[k : k + 1, :] * dot(one_hot(near[:, k : k + 1] == lanes), window)
        total[pl.ds(half * part, half), :] = value
    out[...] = total[...]


def conv_rims(where_ref, low, high, inside, nb_t, ker, zrow, out, halo, merged, *, scene):
    rows, channels = inside.shape
    offsets = nb_t.shape[0]
    halo[pl.ds(0, HALO), :] = low[...]
    halo[pl.ds(HALO, HALO), :] = high[...]
    index = neighbour_rows(nb_t, where_ref[0] * rows, -(4 * rows), scene)
    below, above = index[:HALO, :], index[rows - HALO :, :]
    below = jnp.where(below < 0, below + HALO, -1)
    above = jnp.where(above >= rows, above - rows + HALO, -1)
    near = jnp.concatenate([below, above], axis=0)
    wide = ker[...].astype(f32)
    lanes = iota((2 * HALO, 2 * HALO), 1)
    value = jnp.concatenate([inside[pl.ds(0, HALO), :], inside[pl.ds(rows - HALO, HALO), :]], axis=0)
    for k in range(offsets):
        value = value + wide[k : k + 1, :] * dot(one_hot(near[:, k : k + 1] == lanes), halo[...])
    merged[...] = inside[...].astype(bf16)
    merged[pl.ds(0, HALO), :] = value[:HALO].astype(bf16)
    merged[pl.ds(rows - HALO, HALO), :] = value[HALO:].astype(bf16)
    out[...] = pack_rows(merged[...], slots_by(zrow[...], rows, 0, True))


def first_norm(where_ref, arrived, hrow, gain, weight, ordered, shaped_out, qkv):
    rows, channels = ordered.shape
    points = unpack_rows(arrived[...], slots_by(hrow[...], rows, 1, False))
    ordered[...] = points.astype(bf16)
    normed, _ = normalize(points)
    shaped = (normed * gain[...]).astype(bf16)
    shaped_out[...] = shaped
    result = dot(shaped, weight[...]).astype(bf16)
    here = where_ref[1]
    width = channels // GROUP
    for group in range(GROUP):
        place = lax.rem(group - here + GROUP, GROUP)
        for kind in range(3):
            first = kind * channels + group * width
            qkv[place, :, kind * width : (kind + 1) * width] = result[:, first : first + width]


def attention_forward(b0, b1, b2, b3, probs, out_t, a0, a1, a2, a3, q_all, k_all, v_t, bound):
    head = pl.program_id(0)
    blocks = (b0, b1, b2, b3)
    rows = b0.shape[0]
    width = b0.shape[1] // 3
    keys = rows * GROUP
    factor = HEAD ** (-0.5)

    @pl.when(head == 0)
    def _():
        for place, block in enumerate(blocks):
            here = pl.ds(place * rows, rows)
            q_all[here, :] = (block[:, :width].astype(f32) * factor).astype(bf16)
            k_all[here, :] = block[:, width : 2 * width]
            v_t[:, place * rows : (place + 1) * rows] = block[:, 2 * width :].astype(f32).T.astype(bf16)
        groups = one_hot(iota((width, width), 0) // HEAD == iota((width, width), 1))
        lengths = []
        for ref in (q_all, k_all):
            wide = ref[...].astype(f32)
            lengths.append(jnp.max(dot((wide * wide).astype(bf16), groups), axis=0, keepdims=True))
        bound[0] = jnp.max(lengths[0] * lengths[1])

    mine = (iota((keys, width), 1) // HEAD) == head
    k_head = jnp.where(mine, k_all[...], jnp.zeros((), bf16))
    at = pl.multiple_of(head * HEAD, HEAD)
    v_head = v_t[pl.ds(at, HEAD), :]

    def softmax(shifted, parts):
        for part in range(parts):
            cols = slice(part * (keys // parts), (part + 1) * (keys // parts))
            scores = against(k_head, q_all[cols, :])
            if shifted:
                scores = scores - jnp.max(scores, axis=0, keepdims=True)
            exponent = jnp.exp(scores)
            inverse = 1.0 / jnp.sum(exponent, axis=0, keepdims=True)
            chance = (exponent * inverse).astype(bf16)
            probs[0, :, cols] = chance
            out_t[pl.ds(at, HEAD), cols] = dot(v_head, chance)

    calm = bound[0] <= 1500.0

    @pl.when(calm)
    def _():
        softmax(False, 1)

    @pl.when(jnp.logical_not(calm))
    def _():
        softmax(True, 4)

    @pl.when(head == pl.num_programs(0) - 1)
    def _():
        for place, result in enumerate((a0, a1, a2, a3)):
            result[...] = out_t[:, place * rows : (place + 1) * rows].T.astype(bf16)


def attention_backward(
    b0, b1, b2, b3, u0, u1, u2, u3, probs, out_t, g0, g1, g2, g3,
    q_all, k_all, v_all, u_all, k_t, spread_t, dq_t, dk, dv,
):
    head = pl.program_id(0)
    blocks = (b0, b1, b2, b3)
    rows = b0.shape[0]
    width = b0.shape[1] // 3
    keys = rows * GROUP
    factor = HEAD ** (-0.5)

    @pl.when(head == 0)
    def _():
        for place, (block, up) in enumerate(zip(blocks, (u0, u1, u2, u3))):
            here = pl.ds(place * rows, rows)
            cols = slice(place * rows, (place + 1) * rows)
            q_all[here, :] = block[:, :width]
            k_all[here, :] = block[:, width : 2 * width]
            v_all[here, :] = (block[:, 2 * width :].astype(f32) * factor).astype(bf16)
            u_all[here, :] = up[...]
            k_t[:, cols] = block[:, width : 2 * width].astype(f32).T.astype(bf16)
            spread_t[:, cols] = up[...].astype(f32).T * out_t[:, cols] * factor
        dk[...] = jnp.zeros_like(dk)
        dv[...] = jnp.zeros_like(dv)

    mine = (iota((keys, width), 1) // HEAD) == head
    nought = jnp.zeros((), bf16)
    v_head = jnp.where(mine, v_all[...], nought)
    at = pl.multiple_of(head * HEAD, HEAD)
    k_head = k_t[pl.ds(at, HEAD), :]
    for part in range(GROUP):
        cols = slice(part * rows, (part + 1) * rows)
        chance = probs[0, :, cols]
        grad = against(v_head, u_all[cols, :])
        spread = jnp.sum(spread_t[pl.ds(at, HEAD), cols], axis=0, keepdims=True)
        grad_scores = (chance.astype(f32) * (grad - spread)).astype(bf16)
        own = mine[:rows, :]
        dv[...] += dot(chance, jnp.where(own, u_all[cols, :], nought))
        dk[...] += dot(grad_scores, jnp.where(own, q_all[cols, :], nought))
        dq_t[pl.ds(at, HEAD), cols] = dot(k_head, grad_scores)

    @pl.when(head == pl.num_programs(0) - 1)
    def _():
        for place, result in enumerate((g0, g1, g2, g3)):
            here = pl.ds(place * rows, rows)
            result[:, :width] = dq_t[:, place * rows : (place + 1) * rows].T.astype(bf16)
            result[:, width : 2 * width] = dk[here, :].astype(bf16)
            result[:, 2 * width :] = dv[here, :].astype(bf16)


def mlp(
    where_ref, a0, a1, a2, a3, ordered, first_shaped, out_w, gain, cot, up, down, grad_active,
    mixed, grad_between, upstream, gain_grad, pack, kept,
    between, shaped, normed, scale, sum_mixed, sum_grad,
):
    step = pl.program_id(0)
    rows, channels = ordered.shape
    width = channels // GROUP
    here, core = where_ref[1], where_ref[3]
    chunk = up.shape[1]
    hidden_width = chunk * 4
    right = 3 * channels + hidden_width

    @pl.when(step == 0)
    def _():
        for place, block in enumerate((a0, a1, a2, a3)):
            group = lax.rem(here + place, GROUP)
            pack[:, pl.ds(pl.multiple_of(group * width, width), width)] = block[...]
        attended = pack[:, :channels]
        total = (ordered[...].astype(f32) + dot(attended, out_w[...])).astype(bf16).astype(f32)
        between[...] = total
        normed_value, scale_value = normalize(total)
        normed[...] = normed_value
        scale[...] = jnp.broadcast_to(scale_value, scale.shape)
        shaped_value = (normed_value * gain[...]).astype(bf16)
        shaped[...] = shaped_value
        pack[:, channels : 2 * channels] = shaped_value
        pack[:, 2 * channels + hidden_width : right] = first_shaped[...]
        sum_mixed[...] = total
        sum_grad[...] = jnp.zeros_like(sum_grad)
        half = channels // 2
        at = right + (channels + hidden_width) // 2
        kept[:, (channels + hidden_width) // 2 :] = cot[:, pl.ds(pl.multiple_of(core * half, half), half)]
        pack[:, at:] = cot[:, pl.ds(pl.multiple_of((1 - core) * half, half), half)]

    hidden = dot(shaped[...], up[...])
    activation, derivative = gelu_parts(hidden)
    active = activation.astype(bf16)
    pack[:, pl.ds(pl.multiple_of(2 * channels + step * chunk, chunk), chunk)] = active
    sum_mixed[...] += dot(active, down[...])
    back = (grad_active[...] * derivative).astype(bf16)
    sum_grad[...] += against(back, up[...])
    place = channels // 2 + lax.rem(step, 2) * chunk
    owner = step // 2

    @pl.when(owner == core)
    def _():
        kept[:, pl.ds(pl.multiple_of(place, 128), chunk)] = back

    @pl.when(owner != core)
    def _():
        pack[:, pl.ds(pl.multiple_of(right + place, 128), chunk)] = back

    @pl.when(step == pl.num_programs(0) - 1)
    def _():
        mixed[...] = sum_mixed[...].astype(bf16)
        grad_second = sum_grad[...]
        gain_grad[...] = jnp.sum(grad_second * normed[...], axis=0, keepdims=True)
        grad = norm_back(grad_second, normed[...], scale[:, :1], gain[...]) + cot[...].astype(f32)
        grad = grad.astype(bf16)
        grad_between[...] = grad
        half = channels // 2
        kept[:, :half] = grad_between[:, pl.ds(pl.multiple_of(core * half, half), half)]
        pack[:, right : right + half] = grad_between[:, pl.ds(pl.multiple_of((1 - core) * half, half), half)]
        result = against(grad, out_w[...]).astype(bf16)
        for group in range(GROUP):
            place = lax.rem(group - here + GROUP, GROUP)
            upstream[place, :, :] = result[:, group * width : (group + 1) * width]


def qkv_backward(
    where_ref, g0, g1, g2, g3, ordered, weight, gain, grad_between, hrow,
    kept, sent, homeward, gain_grad, grad_qkv,
):
    rows, channels = ordered.shape
    width = channels // GROUP
    here, core = where_ref[1], where_ref[3]
    for place, block in enumerate((g0, g1, g2, g3)):
        group = lax.rem(here + place, GROUP)
        for kind in range(3):
            first = pl.multiple_of(kind * channels + group * width, width)
            grad_qkv[:, pl.ds(first, width)] = block[:, kind * width : (kind + 1) * width]
    grad_first = against(grad_qkv[...], weight[...])
    normed, scale = normalize(ordered[...].astype(f32))
    gain_grad[...] = jnp.sum(grad_first * normed, axis=0, keepdims=True)
    grad = norm_back(grad_first, normed, scale, gain[...]) + grad_between[...].astype(f32)
    homeward[...] = pack_rows(grad.astype(bf16), slots_by(hrow[...], rows, 0, False))
    half = 3 * channels // 2
    kept[...] = grad_qkv[:, pl.ds(pl.multiple_of(core * half, 128), half)]
    sent[...] = grad_qkv[:, pl.ds(pl.multiple_of((1 - core) * half, 128), half)]


def fold_rows(product):
    rows, columns = product.shape
    half = columns // 2
    tiles = product.reshape(rows // 8, 8, columns)
    turned = pltpu.roll(tiles, 4, 1)
    above = iota((rows // 8, 8, half), 1) < 4
    even = jnp.where(above, tiles[:, :, :half], turned[:, :, half:])
    odd = jnp.where(above, turned[:, :, :half], tiles[:, :, half:])
    return even, odd


def place_folded(out, folded, first, chunk):
    even, odd = folded
    span = even.shape[2]
    for level in range(2):
        for y in range(GROUP):
            q = level * 8 + y * 2
            tall = jnp.concatenate([even[q], odd[q], even[q + 1], odd[q + 1]], axis=0)
            at = (2 * chunk + level) * 32
            out[y, at : at + 32, first : first + span] = tall.astype(bf16)


def hand_out(pieces, here, own, up, down, far_up, far_down):
    half = far_up.shape[0]
    own[...] = pieces[here]
    up[...] = pieces[lax.rem(here + 1, GROUP)]
    down[...] = pieces[lax.rem(here + 3, GROUP)]
    far = lax.rem(here + 2, GROUP)
    far_up[...] = pieces[far, :half, :]
    far_down[...] = pieces[far, half:, :]


def relay(up, down, from_below, from_above, out_up, out_down):
    half = from_below.shape[0]
    out_up[:half, :] = (up[:half, :].astype(f32) + from_below[...].astype(f32)).astype(bf16)
    out_up[half:, :] = up[half:, :]
    out_down[:half, :] = down[:half, :]
    out_down[half:, :] = (down[half:, :].astype(f32) + from_above[...].astype(f32)).astype(bf16)


def early_products(where_ref, pack, kept, came, own, up, down, far_up, far_down, out, *, channels):
    here = where_ref[2]
    hidden_width = pack.shape[1] - kept.shape[1] - 3 * channels
    right = 3 * channels + hidden_width
    half_out, half_up = channels // 2, hidden_width // 2

    def product(left, first, span):
        return contract(pack[:, left], kept[:, first : first + span]) + contract(
            came[:, left], came[:, right + first : right + first + span]
        )

    for chunk in range(4):
        at = chunk * 128
        part = product(slice(at, at + 128), 0, half_out)
        place_folded(out, fold_rows(part), 0, chunk)
        part = product(slice(channels + at, channels + at + 128), half_out, half_up)
        place_folded(out, fold_rows(part), half_out // 2, chunk)
        at = 2 * channels + chunk * 512
        part = product(slice(at, at + 512), half_out + half_up, half_out)
        tiles = part.reshape(32, 2, 8, half_out)
        first = (half_out + half_up) // 2
        for level in range(2):
            for y in range(GROUP):
                q = level * 16 + y * 4
                row = (2 * chunk + level) * 32
                for side in range(2):
                    flat = tiles[q : q + 4, side].reshape(32, half_out).astype(bf16)
                    out[y, row : row + 32, first + side * half_out : first + (side + 1) * half_out] = flat
    hand_out(out, here, own, up, down, far_up, far_down)


def late_products(where_ref, pack, came_pack, kept, came, own, up, down, far_up, far_down, out, *, channels):
    here = where_ref[2]
    for chunk in range(4):
        at = slice(chunk * 128, chunk * 128 + 128)
        part = contract(pack[:, at], kept[...]) + contract(came_pack[:, at], came[...])
        place_folded(out, fold_rows(part), 0, chunk)
    hand_out(out, here, own, up, down, far_up, far_down)


def conv_backward(
    where_ref, returned, low, own, high, nb_t, ker, zrow, first_part, second_part,
    rim_low, rim_high, centre, small, extended, total, *, scene,
):
    rows, channels = own.shape
    offsets = nb_t.shape[0]
    extended[pl.ds(0, HALO), :] = low[...].astype(f32)
    extended[pl.ds(HALO, rows), :] = own[...].astype(f32)
    extended[pl.ds(HALO + rows, HALO), :] = high[...].astype(f32)
    grad_wide = unpack_rows(returned[...], slots_by(zrow[...], rows, 1, True))
    grad = grad_wide.astype(bf16)
    base = where_ref[0] * rows - HALO
    index = nb_t[...]
    index = jnp.where(index == scene, -1, index - base)
    span = rows + 2 * HALO
    sublanes = iota((span, rows), 0)
    wide = ker[...].astype(f32)
    total[...] = jnp.zeros_like(total)
    for k in range(offsets):
        spread = dot(one_hot(index[k : k + 1, :] == sublanes), grad)
        total[...] += wide[k : k + 1, :] * spread
        small[pl.ds(k, 1), :] = jnp.sum(extended[...] * spread, axis=0, keepdims=True)
    small[pl.ds(offsets, 1), :] = first_part[...]
    small[pl.ds(offsets + 1, 1), :] = second_part[...]
    rim_low[...] = total[pl.ds(0, HALO), :]
    rim_high[...] = total[pl.ds(HALO + rows, HALO), :]
    centre[...] = total[pl.ds(HALO, rows), :] + grad_wide


def early_total(e0, e1, e2, out):
    out[...] = (e0[...].astype(f32) + (e1[...].astype(f32) + e2[...].astype(f32))).astype(bf16)


def ring_total(early, l0, l1, l2, out):
    span = early.shape[1]
    out[:, :span] = early[...]
    out[:, span:] = (l0[...].astype(f32) + (l1[...].astype(f32) + l2[...].astype(f32))).astype(bf16)


def add_pieces(got, out):
    out[...] = jnp.sum(got[...].astype(f32), axis=0)


def unfold(where_ref, own, other, qkv_out, out_out, up_out, down_out, *, scale):
    core = where_ref[3]
    lower = jnp.where(core == 0, own[...], other[...]) * scale
    upper = jnp.where(core == 0, other[...], own[...]) * scale
    first = 0
    for result in (out_out, up_out):
        quarter = result.shape[1] // 4
        for place, half in enumerate((lower, upper)):
            for side in range(2):
                at = (2 * place + side) * quarter
                result[:, at : at + quarter] = half[4 * side : 4 * side + 4, first : first + quarter]
        first += quarter
    half_width = down_out.shape[1] // 2
    for place, half in enumerate((lower, upper)):
        for side in range(2):
            at = first + side * half_width
            down_out[8 * side : 8 * side + 8, place * half_width : (place + 1) * half_width] = half[
                :, at : at + half_width
            ]
    first += 2 * half_width
    quarter = qkv_out.shape[1] // 4
    for place, half in enumerate((lower, upper)):
        for side in range(2):
            at = (2 * place + side) * quarter
            qkv_out[:, at : at + quarter] = half[4 * side : 4 * side + 4, first : first + quarter]


def vmem():
    return pl.BlockSpec(memory_space=pltpu.VMEM)


def smem():
    return pl.BlockSpec(memory_space=pltpu.SMEM)


def shape(dims, dtype):
    return jax.ShapeDtypeStruct(dims, dtype)


def call(kernel, outs, inputs, scratch=(), limit=16, grid=None, in_specs=None, out_specs=None, name=None):
    return pl.pallas_call(
        kernel,
        out_shape=tuple(outs),
        in_specs=in_specs or [smem()] + [vmem()] * (len(inputs) - 1),
        out_specs=tuple(out_specs or [vmem()] * len(outs)),
        scratch_shapes=list(scratch),
        compiler_params=pltpu.CompilerParams(vmem_limit_bytes=limit * MB),
        name=name,
        **({} if grid is None else {"grid": grid}),
    )(*inputs)


def around(count, steps, stride=1):
    route = []
    for p in range(count):
        place = p // stride % GROUP
        route.append((p, p + ((place + steps) % GROUP - place) * stride))
    return route


def on_device(
    features, neighbours, z_to_hilbert, hilbert, conv_kernel, first_gain, second_gain,
    qkv_weight, out_weight, up_weight, down_weight, cotangent,
):
    points = features[0]
    rows, channels = points.shape
    devices = lax.axis_size("pts")
    device = lax.axis_index("pts")
    core = lax.axis_index("rep")
    replicas = lax.axis_size("rep")
    scene = rows * devices
    width = channels // GROUP
    hidden_width = up_weight.shape[1]
    offsets = neighbours.shape[2]
    patch = rows * GROUP
    group_heads = HEADS // GROUP
    where = jnp.stack([device, device % GROUP, device // GROUP % GROUP, core]).astype(jnp.int32)
    forward = [(i, i + 1) for i in range(devices - 1)]
    backward = [(i + 1, i) for i in range(devices - 1)]
    swap = [(0, 1), (1, 0)]
    low = lax.ppermute(points[rows - HALO :], "pts", forward)
    high = lax.ppermute(points[:HALO], "pts", backward)
    nb_t = neighbours[0].T
    gain1, gain2 = first_gain.reshape(1, channels), second_gain.reshape(1, channels)
    incoming = cotangent[0]

    (inside,) = call(
        functools.partial(conv_inside, scene=scene),
        [shape((rows, channels), f32)],
        (where, points, nb_t, conv_kernel),
        [pltpu.VMEM((rows, channels), f32)],
        name="conv_inside",
    )
    (outgoing,) = call(
        functools.partial(conv_rims, scene=scene),
        [shape((4 * rows, channels // 2), bf16)],
        (where, low, high, inside, nb_t, conv_kernel, z_to_hilbert),
        [pltpu.VMEM((2 * HALO, channels), bf16), pltpu.VMEM((rows, channels), bf16)],
        name="conv_rims",
    )

    def exchange(value):
        cut = value.reshape(devices, 2 * SLOTS, channels // 2)
        got = lax.all_to_all(cut, "pts", split_axis=0, concat_axis=0, tiled=True)
        return got.reshape(4 * rows, channels // 2)

    arrived = exchange(outgoing)
    grad_active = against(incoming, down_weight)

    ordered, shaped1, qkv = call(
        first_norm,
        [shape((rows, channels), bf16), shape((rows, channels), bf16), shape((GROUP, rows, 3 * width), bf16)],
        (where, arrived, hilbert, gain1, qkv_weight),
        name="first_norm",
    )

    def spread_out(blocks, stride=1):
        return [blocks[0]] + [lax.ppermute(blocks[j], "pts", around(devices, j, stride)) for j in range(1, GROUP)]

    def bring_back(blocks):
        return [blocks[0]] + [lax.ppermute(blocks[j], "pts", around(devices, -j)) for j in range(1, GROUP)]

    blocks = spread_out(qkv)

    by_head = pl.BlockSpec((1, patch, patch), lambda i: (i, 0, 0))
    probs, out_t, *attended = call(
        attention_forward,
        [shape((group_heads, patch, patch), bf16), shape((width, patch), f32)]
        + [shape((rows, width), bf16)] * GROUP,
        blocks,
        [
            pltpu.VMEM((patch, width), bf16),
            pltpu.VMEM((patch, width), bf16),
            pltpu.VMEM((width, patch), bf16),
            pltpu.SMEM((1,), f32),
        ],
        limit=24,
        grid=(group_heads,),
        in_specs=[vmem()] * GROUP,
        out_specs=[by_head] + [vmem()] * (1 + GROUP),
        name="attention_forward",
    )

    attended = bring_back(attended)

    chunk = hidden_width // 4
    kept_width = (2 * channels + hidden_width) // 2
    pack_width = 3 * channels + hidden_width + kept_width
    mixed_rows, grad_between, upstream, second_gain_part, pack, kept = call(
        mlp,
        [
            shape((rows, channels), bf16),
            shape((rows, channels), bf16),
            shape((GROUP, rows, width), bf16),
            shape((1, channels), f32),
            shape((rows, pack_width), bf16),
            shape((rows, kept_width), bf16),
        ],
        (where, *attended, ordered, shaped1, out_weight, gain2, incoming, up_weight, down_weight, grad_active),
        [
            pltpu.VMEM((rows, channels), f32),
            pltpu.VMEM((rows, channels), bf16),
            pltpu.VMEM((rows, channels), f32),
            pltpu.VMEM((rows, 128), f32),
            pltpu.VMEM((rows, channels), f32),
            pltpu.VMEM((rows, channels), f32),
        ],
        limit=20,
        grid=(4,),
        in_specs=[smem()]
        + [vmem()] * (GROUP + 5)
        + [
            pl.BlockSpec((channels, chunk), lambda i: (0, i)),
            pl.BlockSpec((chunk, channels), lambda i: (i, 0)),
            pl.BlockSpec((rows, chunk), lambda i: (0, i)),
        ],
        name="mlp",
    )

    upper = spread_out(upstream)
    came = lax.ppermute(pack, "rep", swap)
    *upper, came = lax.optimization_barrier((*upper, came))

    def ring_shapes(columns):
        full, half = shape((rows, columns), bf16), shape((rows // 2, columns), bf16)
        return [full, full, full, half, half]

    def step(value, steps):
        return lax.ppermute(value, "pts", around(devices, steps, GROUP))

    def relayed(up, down, below, above):
        return call(
            relay, [shape(up.shape, bf16)] * 2, (up, down, below, above), in_specs=[vmem()] * 4, name="relay"
        )

    columns = 9 * channels // 4
    early_own, up, down, far_up, far_down = call(
        functools.partial(early_products, channels=channels),
        ring_shapes(columns),
        (where, pack, kept, came),
        [pltpu.VMEM((GROUP, rows, columns), bf16)],
        limit=20,
        name="early_products",
    )
    below, above = step(far_up, 1), step(far_down, -1)
    *upper, early_own = lax.optimization_barrier((*upper, early_own))

    grads = call(
        attention_backward,
        [shape((rows, 3 * width), bf16)] * GROUP,
        (*blocks, *upper, probs, out_t),
        [
            pltpu.VMEM((patch, width), bf16),
            pltpu.VMEM((patch, width), bf16),
            pltpu.VMEM((patch, width), bf16),
            pltpu.VMEM((patch, width), bf16),
            pltpu.VMEM((width, patch), bf16),
            pltpu.VMEM((width, patch), f32),
            pltpu.VMEM((width, patch), f32),
            pltpu.VMEM((patch, width), f32),
            pltpu.VMEM((patch, width), f32),
        ],
        limit=24,
        grid=(group_heads,),
        in_specs=[vmem()] * (2 * GROUP) + [by_head, vmem()],
        name="attention_backward",
    )

    *grads, below, above = lax.optimization_barrier((*grads, below, above))
    grads = bring_back(grads)
    up, down = relayed(up, down, below, above)
    below, above = step(up, 1), step(down, -1)
    qkv_kept, qkv_sent, homeward, first_gain_part = call(
        qkv_backward,
        [
            shape((rows, 3 * channels // 2), bf16),
            shape((rows, 3 * channels // 2), bf16),
            shape((4 * rows, channels // 2), bf16),
            shape((1, channels), f32),
        ],
        (where, *grads, ordered, qkv_weight, gain1, grad_between, hilbert),
        [pltpu.VMEM((rows, 3 * channels), bf16)],
        name="qkv_backward",
    )

    (early,) = call(
        early_total, [shape(early_own.shape, bf16)], (early_own, below, above), in_specs=[vmem()] * 3,
        name="early_total",
    )
    homeward, early = lax.optimization_barrier((homeward, early))
    returned = exchange(homeward)
    qkv_came = lax.ppermute(qkv_sent, "rep", swap)
    other_shaped1 = came[:, 2 * channels + hidden_width : 3 * channels + hidden_width]
    columns = 3 * channels // 4
    late_own, up, down, far_up, far_down = call(
        functools.partial(late_products, channels=channels),
        ring_shapes(columns),
        (where, shaped1, other_shaped1, qkv_kept, qkv_came),
        [pltpu.VMEM((GROUP, rows, columns), bf16)],
        name="late_products",
    )
    up, down = relayed(up, down, step(far_up, 1), step(far_down, -1))
    late_parts = (late_own, step(up, 1), step(down, -1))

    rim_low, rim_high, centre, small = call(
        functools.partial(conv_backward, scene=scene),
        [
            shape((HALO, channels), f32),
            shape((HALO, channels), f32),
            shape((rows, channels), f32),
            shape((offsets + 2, channels), f32),
        ],
        (
            where, returned, low, points, high, nb_t, conv_kernel, z_to_hilbert,
            first_gain_part, second_gain_part,
        ),
        [pltpu.VMEM((rows + 2 * HALO, channels), f32), pltpu.VMEM((rows + 2 * HALO, channels), f32)],
        name="conv_backward",
    )

    _, *late_parts = lax.optimization_barrier((small, *late_parts))
    (piece,) = call(
        ring_total, [shape((rows, 3 * channels), bf16)], (early, *late_parts),
        in_specs=[vmem()] * 4, name="ring_total",
    )
    layers = devices // (GROUP * GROUP)
    groups = [
        [z * GROUP * GROUP + y * GROUP + x for z in range(layers) for x in range(GROUP)] for y in range(GROUP)
    ]
    got = lax.all_to_all(
        piece.reshape(devices // GROUP, 8, 3 * channels),
        "pts", split_axis=0, concat_axis=0, axis_index_groups=groups, tiled=True,
    )
    (owned,) = call(
        add_pieces, [shape((8, 3 * channels), f32)], (got,), in_specs=[vmem()], name="add_pieces"
    )
    other = lax.ppermute(owned, "rep", swap)
    scale = 1.0 / math.sqrt(scene * replicas)
    weight_grads = call(
        functools.partial(unfold, scale=scale),
        [
            shape((4, 3 * channels), f32),
            shape((4, channels), f32),
            shape((4, hidden_width), f32),
            shape((down_weight.shape[0] // devices, channels), f32),
        ],
        (where, owned, other),
        name="unfold",
    )

    def partner(value, axis, mask):
        count = replicas if axis == "rep" else devices
        return lax.ppermute(value, axis, [(p, p ^ mask) for p in range(count)])

    bit = 1
    while bit < devices:
        if 4 * bit <= devices:
            near, far, across = [partner(small, "pts", m * bit) for m in (1, 2, 3)]
            small = (small + near) + (far + across)
            bit *= 4
        else:
            small = small + partner(small, "pts", bit)
            bit *= 2
        if bit == GROUP * GROUP:
            small, rim_low, rim_high = lax.optimization_barrier((small, rim_low, rim_high))
    small = (small + partner(small, "rep", 1)) * scale

    from_above = lax.ppermute(rim_low, "pts", backward)
    from_below = lax.ppermute(rim_high, "pts", forward)
    centre = centre.at[:HALO].add(from_below).at[rows - HALO :].add(from_above)
    grad_features = centre.astype(bf16)

    return (
        mixed_rows[None],
        grad_features[None],
        small[:offsets],
        small[offsets],
        small[offsets + 1],
        *weight_grads,
    )


def solution(mesh):
    return jax.shard_map(
        on_device,
        mesh=mesh,
        in_specs=(
            P("rep", "pts", None),
            P("rep", "pts", None),
            P("rep", "pts"),
            P("rep", "pts"),
            P(),
            P(),
            P(),
            P(),
            P(),
            P(),
            P(),
            P("rep", "pts", None),
        ),
        out_specs=(
            P("rep", "pts", None),
            P("rep", "pts", None),
            P(),
            P(),
            P(),
            P("pts", None),
            P("pts", None),
            P("pts", None),
            P("pts", None),
        ),
        check_vma=False,
    )
```
